128 devices in a mesh: seq: 8 (over y_hi, x), exp: 16 (over z, y_lo, core).
Axes of the slice: x: 4, y: 4 (y_hi: 2, y_lo: 2; y = y_hi * 2 + y_lo), z: 4, core: 2. Of those that a mesh axis runs over, the one named last changes fastest.
Arguments:
- tokens: bfloat16 [16, 8192, 1280], P('exp', 'seq'), may hold values from -48 to 48, as said below
- router: bfloat16 [1280, 32], replicated, as said below
- w_in: bfloat16 [32, 1280, 5120], P('exp', None, 'seq'), may hold values from -0.15625 to 0.15625
- w_out: bfloat16 [32, 5120, 1280], P('exp', 'seq'), may hold values from -0.078125 to 0.078125
- grad_out: bfloat16 [16, 8192, 1280], P('exp', 'seq'), may hold values from -6 to 6
Outputs:
- mixed: bfloat16 [16, 8192, 1280], P('exp', 'seq')
- grad_tokens: bfloat16 [16, 8192, 1280], P('exp', 'seq')
- grad_router: float32 [1280, 32], P('seq')
- grad_w_in: bfloat16 [32, 1280, 5120], P('exp', None, 'seq')
- grad_w_out: bfloat16 [32, 5120, 1280], P('exp', 'seq')
The draws below stay inside these ranges and needn't reach their ends.
Inputs may be any that keep to these rules, and one draw needn't show every extreme that they name: tokens are finite and of order one but for a few rows in some draws. `router`: entries are of the order of 2.5 times the inverse square root of 1280.
All inputs are finite; a program needn't handle non-finite values.
Results may differ from the reference program's by a relative error of at most 0.035.
Values may be sent and summed in bfloat16 or wider, within the bound.
No kernel may reach another device: no remote copies, remote signals or barrier semaphores. Data moves between devices by JAX's collectives and lax.ppermute only.
A program may use at most 128 MiB of HBM per device.

```python
import math
import jax
import jax.numpy as jnp
from jax import lax

D = 1280
FF = 5120
EXPERTS = 32
CLIPS = 16
LENGTH = 8192


logit_spread = 2.5


def router_table(key):
    raw = jax.random.truncated_normal(key, -4.0, 4.0, (D, EXPERTS), jnp.float32)
    return raw * (logit_spread / math.sqrt(D))


def draw_router(key, part):
    return router_table(key).astype(jnp.bfloat16)


def draw_tokens(key, part):
    key = jax.random.fold_in(key, 11)
    key_base = jax.random.fold_in(key, 0)
    base = jax.random.truncated_normal(key_base, -6.0, 6.0, (CLIPS, LENGTH, D), jnp.float32)
    return jnp.clip(base, -48.0, 48.0).astype(jnp.bfloat16)


def steps_of(stream_key, extent, pieces, low, top_value):
    factor_of, own = 1.0, jax.random.fold_in(stream_key, 6)
    for position, shards_of in pieces:
        heights = jnp.exp(jax.random.uniform(jax.random.fold_in(own, position), (shards_of,), jnp.float32, low / len(pieces), top_value / len(pieces)))
        factor_of = factor_of * jnp.repeat(heights, extent[position] // shards_of).reshape([-1 if axis == position else 1 for axis in range(len(extent))])
    return factor_of


def scatter_about(key, shape, spread, reach, pieces=(), dtype=jnp.bfloat16):
    result = jax.random.normal(key, shape, jnp.float32) * spread
    if len(pieces) > 0:
        result = steps_of(key, shape, pieces, -0.22, 0.18) * result
    return jnp.clip(result, min=-reach, max=reach).astype(dtype)


def setup_inputs(seed: int = 0) -> dict:
    arg_keys = jax.random.split(jax.random.key(seed), 6)
    return {
        "tokens": draw_tokens(jax.random.fold_in(arg_keys[5], 71), 0),
        "router": draw_router(jax.random.fold_in(arg_keys[5], 71), 0),
        "w_in": scatter_about(arg_keys[2], (EXPERTS, D, FF), D ** -0.5, 0.15625, ((0, 16), (2, 8))),
        "w_out": scatter_about(arg_keys[3], (EXPERTS, FF, D), FF ** -0.5, 0.078125, ((0, 16), (1, 8))),
        "grad_out": scatter_about(arg_keys[4], (CLIPS, LENGTH, D), 1.0, 6.0, ((0, 16), (1, 8))),
    }


def gelu_slope(activation):
    cumulative = 0.5 * (1.0 + lax.erf(activation * (1.0 / math.sqrt(2.0))))
    density = jnp.exp(-0.5 * activation * activation) * (1.0 / math.sqrt(2.0 * math.pi))
    return cumulative + activation * density

def reference(tokens, router, w_in, w_out, grad_out):
    flat_tokens = tokens.reshape(CLIPS * LENGTH, D)
    logits = jnp.dot(flat_tokens, router, preferred_element_type=jnp.float32).reshape(CLIPS, LENGTH, EXPERTS)
    column_top = lax.optimization_barrier(jnp.max(logits, axis=1, keepdims=True))
    weights_raw = jnp.exp(logits - column_top)
    weights_half = weights_raw.astype(jnp.bfloat16)
    denominator = lax.optimization_barrier(jnp.sum(weights_raw, axis=1))
    tokens_wide = tokens.astype(jnp.float32)
    numerator = jnp.einsum('clw,cld->cwd', weights_half.astype(jnp.float32), tokens_wide)
    slot_full = numerator / denominator[:, :, None]
    slot_half = slot_full.astype(jnp.bfloat16)
    routed = slot_half.astype(jnp.float32)
    w_in_wide = w_in.astype(jnp.float32)
    w_out_wide = w_out.astype(jnp.float32)
    activation = jnp.einsum('cwd,wdf->cwf', routed, w_in_wide)
    hidden = jax.nn.gelu(activation, approximate=False).astype(jnp.bfloat16)
    hidden_wide = hidden.astype(jnp.float32)
    slot_out = jnp.einsum('cwf,wfd->cwd', hidden_wide, w_out_wide).astype(jnp.bfloat16)
    slot_out_wide = slot_out.astype(jnp.float32)
    probs = jax.nn.softmax(logits, axis=2)
    probs_half = probs.astype(jnp.bfloat16)
    mixed = jnp.einsum('clw,cwd->cld', probs_half.astype(jnp.float32), slot_out_wide).astype(jnp.bfloat16)
    grad_wide = grad_out.astype(jnp.float32)
    grad_probs = jnp.einsum('cld,cwd->clw', grad_wide, slot_out_wide)
    comb_grad = probs * (grad_probs - lax.optimization_barrier(jnp.sum(probs * grad_probs, axis=2, keepdims=True)))
    slot_grad = jnp.einsum('clw,cld->cwd', probs_half.astype(jnp.float32), grad_wide).astype(jnp.bfloat16)
    slot_grad_wide = slot_grad.astype(jnp.float32)
    hidden_grad = jnp.einsum('cwd,wfd->cwf', slot_grad_wide, w_out_wide)
    grad_w_out = jnp.einsum('cwf,cwd->wfd', hidden_wide, slot_grad_wide).astype(jnp.bfloat16)
    pre_grad = (hidden_grad * gelu_slope(activation)).astype(jnp.bfloat16)
    pre_wide = pre_grad.astype(jnp.float32)
    grad_w_in = jnp.einsum('cwd,cwf->wdf', routed, pre_wide).astype(jnp.bfloat16)
    input_grad = jnp.einsum('cwf,wdf->cwd', pre_wide, w_in_wide)
    in_half = input_grad.astype(jnp.bfloat16)
    in_scaled = (input_grad / denominator[:, :, None]).astype(jnp.bfloat16)
    inner_prod = jnp.einsum('cld,cwd->clw', tokens_wide, in_half.astype(jnp.float32))
    shift_term = lax.optimization_barrier(jnp.sum(weights_half.astype(jnp.float32) * inner_prod, axis=1)) / denominator
    disp_grad = weights_raw / denominator[:, None, :] * (inner_prod - shift_term[:, None, :])
    logit_grad = (comb_grad + disp_grad).astype(jnp.bfloat16)
    token_grad = jnp.einsum('clw,dw->cld', logit_grad.astype(jnp.float32), router.astype(jnp.float32))
    token_grad = token_grad + jnp.einsum('clw,cwd->cld', weights_half.astype(jnp.float32), in_scaled.astype(jnp.float32))
    grad_tokens = token_grad.astype(jnp.bfloat16)
    grad_router = jnp.dot(flat_tokens.T, logit_grad.reshape(CLIPS * LENGTH, EXPERTS), preferred_element_type=jnp.float32)
    return (mixed, grad_tokens, grad_router, grad_w_in, grad_w_out)
```

```python
import math

import jax
import jax.numpy as jnp
from jax import lax
from jax.sharding import Mesh, PartitionSpec as P

bf16 = jnp.bfloat16
f32 = jnp.float32
ALL = ("yh", "x", "z", "yl", "core")
SEQ = ("yh", "x")
EXP = ("z", "yl", "core")
EXTRA = 128


def gelu_slope(activation):
    cumulative = 0.5 * (1.0 + lax.erf(activation * (1.0 / math.sqrt(2.0))))
    density = jnp.exp(-0.5 * activation * activation) * (1.0 / math.sqrt(2.0 * math.pi))
    return cumulative + activation * density


def pieces(value):
    high = lax.reduce_precision(value, 8, 7)
    rest = value - high
    middle = lax.reduce_precision(rest, 8, 7)
    low = rest - middle
    return jnp.stack([high, middle, low], axis=-1).astype(bf16)


def joined(parts):
    wide = parts.astype(f32)
    return wide[..., 0] + wide[..., 1] + wide[..., 2]


def padded(parts):
    return jnp.pad(parts, [(0, 0)] * (parts.ndim - 1) + [(0, EXTRA - parts.shape[-1])])


def per_device(tokens, router, w_in, w_out, grad_out):
    x_index = lax.axis_index("x")
    own_slot = x_index // 2
    own_array = x_index % 2
    tok = tokens[0]
    grad = grad_out[0]
    width = router.shape[0]
    slots = router.shape[1]
    held = w_in.shape[0]
    owners = slots // held
    router_t = router.T.reshape(owners, held, width).swapaxes(0, 1).reshape(slots, width)
    logits = jnp.einsum("wd,td->wt", router_t, tok, preferred_element_type=f32)
    top = jnp.max(logits, axis=1, keepdims=True)
    weights = jnp.exp(logits - top)
    total = jnp.sum(weights, axis=1, keepdims=True)
    local_slot = jnp.dot(weights.astype(bf16), tok, preferred_element_type=f32) / total
    local_lse = (top + jnp.log(total))[:, 0]
    probs = jax.nn.softmax(logits, axis=0)
    probs_half = probs.astype(bf16)
    local_grad = jnp.dot(probs_half, grad, preferred_element_type=f32)
    rows = jnp.stack(
        [local_slot.reshape(held, owners, width), local_grad.reshape(held, owners, width)], axis=1
    ).astype(bf16)
    rows = rows.reshape(2 * held, owners, width)
    extra = padded(pieces(local_lse.reshape(held, owners).T).reshape(owners, 3 * held))
    send = jnp.concatenate(
        [rows, jnp.broadcast_to(extra[None], (2 * held, owners, EXTRA))], axis=2
    )
    got = lax.all_to_all(send, "x", 0, 0, tiled=True)
    lse_x = joined(got[:, :, width : width + 3 * held].reshape(4, owners, held, 3))
    lse_own = lax.dynamic_index_in_dim(lse_x, own_slot, 2, keepdims=False)
    lse_sum = jax.nn.logsumexp(lse_own, axis=0)
    scale = jnp.where(own_array == 0, jnp.exp(lse_own - lse_sum[None]), 1.0)
    row = jnp.sum(got[:, :, :width].astype(f32) * scale[:, :, None], axis=0).astype(bf16)
    row = jnp.concatenate([row, padded(pieces(lse_sum))], axis=1)
    wide = width + EXTRA
    send = jnp.broadcast_to(row[None], (8, owners, wide)).reshape(8 * owners, wide)
    got = lax.all_to_all(send, ALL, 0, 0, tiled=True).reshape(2, held, 2, owners, wide)
    lse_y = joined(got[:, :, 0, :, width : width + 3])
    lse = jax.nn.logsumexp(lse_y, axis=0)
    scale = jnp.exp(lse_y - lse[None])
    slot_half = jnp.sum(got[:, :, 0, :, :width].astype(f32) * scale[..., None], axis=0).astype(bf16)
    slot_grad = jnp.sum(got[:, :, 1, :, :width].astype(f32), axis=0).astype(bf16)
    activation = jnp.einsum("kce,kef->kcf", slot_half, w_in, preferred_element_type=f32)
    hidden = jax.nn.gelu(activation, approximate=False).astype(bf16)
    partial_out = jnp.einsum("kcf,kfd->kcd", hidden, w_out, preferred_element_type=f32)
    hidden_grad = jnp.einsum("kcd,kfd->kcf", slot_grad, w_out, preferred_element_type=f32)
    pre_grad = (hidden_grad * gelu_slope(activation)).astype(bf16)
    partial_in = jnp.einsum("kcf,kef->kce", pre_grad, w_in, preferred_element_type=f32)
    send = jnp.stack([partial_out, partial_in], axis=1).astype(bf16).reshape(2 * held, owners, width)
    got = lax.all_to_all(send, "x", 0, 0, tiled=True)
    grad_w_out = jnp.einsum(
        "kcf,kcd->kfd", hidden, slot_grad, preferred_element_type=f32
    ).astype(bf16)
    grad_w_in = jnp.einsum(
        "kce,kcf->kef", slot_half, pre_grad, preferred_element_type=f32
    ).astype(bf16)
    row = jnp.sum(got.astype(f32), axis=0).astype(bf16)
    own_half = lax.dynamic_index_in_dim(slot_half, own_slot, 0, keepdims=False).astype(f32)
    own_lse = lax.dynamic_index_in_dim(lse, own_slot, 0, keepdims=False)
    shift = jnp.sum(own_half * row.astype(f32), axis=1)
    extra = padded(jnp.concatenate([pieces(own_lse), pieces(shift)], axis=1))
    row = jnp.concatenate([row, extra], axis=1)
    send = jnp.broadcast_to(row[None], (8, owners, wide)).reshape(8 * owners, wide)
    got = lax.all_to_all(send, ALL, 0, 0, tiled=True).reshape(2, held, 2, owners, wide)
    summed = jnp.sum(got[..., :width].astype(f32), axis=0).astype(bf16)
    slot_out = summed[:, 0].reshape(slots, width)
    in_half = summed[:, 1].reshape(slots, width)
    lse = joined(got[0, :, 0, :, width : width + 3]).reshape(slots, 1)
    shift = jnp.sum(joined(got[:, :, 1, :, width + 3 : width + 6]), axis=0).reshape(slots, 1)
    grad_probs = jnp.einsum("wd,td->wt", slot_out, grad, preferred_element_type=f32)
    comb_grad = probs * (grad_probs - jnp.sum(probs * grad_probs, axis=0, keepdims=True))
    share = jnp.exp(logits - lse)
    inner = jnp.einsum("wd,td->wt", in_half, tok, preferred_element_type=f32)
    logit_grad = (comb_grad + share * (inner - shift)).astype(bf16)
    router_local = jnp.dot(logit_grad, tok, preferred_element_type=f32)
    router_local = router_local.reshape(held, owners, 8, 16, width // 128).transpose(2, 3, 4, 1, 0)
    got = lax.all_to_all(
        router_local.reshape(128, width // 128 * slots), ALL, 0, 0, tiled=True
    )
    part = jnp.sum(got, axis=0)
    mixed = jnp.einsum("wt,wd->td", probs_half, slot_out, preferred_element_type=f32).astype(bf16)
    both = jnp.concatenate([logit_grad, share.astype(bf16)], axis=0)
    table = jnp.concatenate([router_t, in_half], axis=0)
    grad_tokens = jnp.einsum("wt,wd->td", both, table, preferred_element_type=f32).astype(bf16)
    got = lax.all_to_all(
        jnp.broadcast_to(part[None], (16, part.shape[0])), EXP, 0, 0, tiled=True
    )
    grad_router = got.reshape(width // 8, slots)
    return (mixed[None], grad_tokens[None], grad_router, grad_w_in, grad_w_out)


def solution(mesh):
    fine = Mesh(mesh.devices.reshape(2, 4, 4, 2, 2), ALL)
    in_specs = (
        P(EXP, SEQ, None),
        P(),
        P(EXP, None, SEQ),
        P(EXP, SEQ, None),
        P(EXP, SEQ, None),
    )
    out_specs = (
        P(EXP, SEQ, None),
        P(EXP, SEQ, None),
        P(SEQ, None),
        P(EXP, None, SEQ),
        P(EXP, SEQ, None),
    )
    return jax.shard_map(
        per_device, mesh=fine, in_specs=in_specs, out_specs=out_specs, check_vma=False
    )
```

```python
import math

import jax
import jax.numpy as jnp
from jax import lax
from jax.experimental import pallas as pl
from jax.experimental.pallas import tpu as pltpu
from jax.sharding import Mesh, PartitionSpec as P

bf16 = jnp.bfloat16
f32 = jnp.float32
ALL = ("yh", "x", "z", "yl", "core")
SEQ = ("yh", "x")
EXP = ("z", "yl", "core")
CHIPS = ("yh", "x", "z", "yl")
LANES = 128
CHUNKS = 4
MIB = 1024 * 1024

VMEM = pl.BlockSpec(memory_space=pltpu.VMEM)
SMEM = pl.BlockSpec(memory_space=pltpu.SMEM)
HBM = pl.BlockSpec(memory_space=pl.ANY)


def nn(a, b):
    return jnp.dot(a, b, preferred_element_type=f32)


def nt(a, b):
    return lax.dot_general(a, b, (((1,), (1,)), ((), ())), preferred_element_type=f32)


def tn(a, b):
    return lax.dot_general(a, b, (((0,), (0,)), ((), ())), preferred_element_type=f32)


def shape(dims, dtype):
    return jax.ShapeDtypeStruct(dims, dtype)


def cost(flops, moved):
    return pl.CostEstimate(flops=flops, bytes_accessed=moved, transcendentals=0)


def pieces(value):
    high = value.astype(bf16).astype(f32)
    rest = value - high
    middle = rest.astype(bf16).astype(f32)
    return high, middle, rest - middle


def in_lanes(columns):
    rows = columns[0].shape[0]
    lane = lax.broadcasted_iota(jnp.int32, (rows, LANES), 1)
    result = jnp.zeros((rows, LANES), f32)
    for place, column in enumerate(columns):
        result = jnp.where(lane == place, column, result)
    return result


def from_lanes(block, first):
    lane = lax.broadcasted_iota(jnp.int32, block.shape, 1)
    kept = jnp.where((lane >= first) & (lane < first + 3), block, 0.0)
    return jnp.sum(kept, axis=1, keepdims=True)


def log_sum_exp(values):
    top = values[0]
    for value in values[1:]:
        top = jnp.maximum(top, value)
    total = jnp.exp(values[0] - top)
    for value in values[1:]:
        total = total + jnp.exp(value - top)
    return top + jnp.log(total)


def normal(value):
    return 0.5 * (1.0 + lax.erf(value * (1.0 / math.sqrt(2.0))))


def router_rows(router_ref, owners, held):
    slots = owners * held
    row = lax.broadcasted_iota(jnp.int32, (slots, slots), 0)
    column = lax.broadcasted_iota(jnp.int32, (slots, slots), 1)
    order = (column == (row % owners) * held + row // owners).astype(bf16)
    return nt(order, router_ref[...]).astype(bf16)


def slot_softmax(logits):
    top = jnp.max(logits, axis=0, keepdims=True)
    raw = jnp.exp(logits - top)
    return raw / jnp.sum(raw, axis=0, keepdims=True)


def first_kernel(
    x_ref, tok_ref, router_ref, grad_ref, out0, out1, out2, out3, logits_ref,
    tok, grad, held_rows, sems,
):
    length, width = tok_ref.shape
    slots = router_ref.shape[1]
    owners = out0.shape[0]
    held = slots // owners
    chunk = length // CHUNKS
    copies = []
    for source, target, first in ((tok_ref, tok, 0), (grad_ref, grad, CHUNKS)):
        for part in range(CHUNKS):
            rows = pl.ds(part * chunk, chunk)
            copies.append(
                pltpu.make_async_copy(
                    source.at[rows, :], target.at[rows, :], sems.at[first + part]
                )
            )
    for copy in copies:
        copy.start()
    table = router_rows(router_ref, owners, held)
    for part in range(CHUNKS):
        copies[part].wait()
        rows = pl.ds(part * chunk, chunk)
        logits_ref[:, rows] = nt(table, tok[rows, :])
    logits = logits_ref[...]
    top = jnp.max(logits, axis=1, keepdims=True)
    raw = jnp.exp(logits - top)
    total = jnp.sum(raw, axis=1, keepdims=True)
    local_slot = nn(raw.astype(bf16), tok[...]) / total
    lse = top + jnp.log(total)
    probs = slot_softmax(logits).astype(bf16)
    for copy in copies[CHUNKS:]:
        copy.wait()
    local_grad = nn(probs, grad[...])
    columns = []
    for place in range(held):
        columns += pieces(lse[place * owners : (place + 1) * owners])
    extra = in_lanes(columns).astype(bf16)
    for place in range(held):
        for array, value in enumerate((local_slot, local_grad)):
            quarter = place * 2 + array
            rows = value[place * owners : (place + 1) * owners]
            held_rows[quarter, :, :width] = rows.astype(bf16)
            held_rows[quarter, :, width:] = extra
    x = x_ref[0]
    for turn, out in enumerate((out0, out1, out2, out3)):
        out[...] = held_rows[(x + turn) % 4]


def write_rows(out_ref, row, extra):
    owners, width = row.shape
    half = width // 2
    halves = [
        jnp.concatenate([row[:, :half], extra], axis=1),
        jnp.concatenate([row[:, half:], extra], axis=1),
    ]
    both = jnp.stack(halves, axis=1).astype(bf16)
    for member in range(out_ref.shape[0] // owners):
        out_ref[member * owners : (member + 1) * owners] = both


def read_rows(got_ref, member, owners):
    first = member * owners
    half = got_ref.shape[2] - LANES
    left = got_ref[first : first + owners, 0, :].astype(f32)
    right = got_ref[first : first + owners, 1, :].astype(f32)
    return jnp.concatenate([left[:, :half], right[:, :half]], axis=1), left[:, half:]


def first_sum_kernel(x_ref, in0, in1, in2, in3, out_ref):
    width = in0.shape[1] - LANES
    x = x_ref[0]
    blocks = [ref[...].astype(f32) for ref in (in0, in1, in2, in3)]
    lses = []
    for block in blocks:
        extra = block[:, width:]
        lses.append(jnp.where(x // 2 == 0, from_lanes(extra, 0), from_lanes(extra, 3)))
    lse = log_sum_exp(lses)
    row = None
    for block, part in zip(blocks, lses):
        scale = jnp.where(x % 2 == 0, jnp.exp(part - lse), 1.0)
        term = block[:, :width] * scale
        row = term if row is None else row + term
    write_rows(out_ref, row, in_lanes(pieces(lse)))


def expert_kernel(
    x_ref, got_ref, w_in_ref, w_out_ref,
    out0, out1, out2, out3, slot_ref, slot_grad_ref, hidden_ref, pre_ref, lse_ref, held_rows,
):
    held = w_in_ref.shape[0]
    owners = out0.shape[0]
    for place in range(held):
        rows, lses = [], []
        for y in range(2):
            data, extra = read_rows(got_ref, y * 4 + place * 2, owners)
            rows.append(data)
            lses.append(from_lanes(extra, 0))
        lse = log_sum_exp(lses)
        slot = (
            rows[0] * jnp.exp(lses[0] - lse) + rows[1] * jnp.exp(lses[1] - lse)
        ).astype(bf16)
        grads = [read_rows(got_ref, y * 4 + place * 2 + 1, owners)[0] for y in range(2)]
        slot_grad = (grads[0] + grads[1]).astype(bf16)
        slot_ref[place] = slot
        slot_grad_ref[place] = slot_grad
        lse_ref[place] = in_lanes(pieces(lse))
        activation = nn(slot, w_in_ref[place])
        hidden_grad = nt(slot_grad, w_out_ref[place])
        cumulative = normal(activation)
        density = jnp.exp(-0.5 * activation * activation) * (1.0 / math.sqrt(2.0 * math.pi))
        hidden = (activation * cumulative).astype(bf16)
        pre = (hidden_grad * (cumulative + activation * density)).astype(bf16)
        hidden_ref[place] = hidden
        pre_ref[place] = pre
        held_rows[place * 2] = nn(hidden, w_out_ref[place]).astype(bf16)
        held_rows[place * 2 + 1] = nt(pre, w_in_ref[place]).astype(bf16)
    x = x_ref[0]
    for turn, out in enumerate((out0, out1, out2, out3)):
        out[...] = held_rows[(x + turn) % 4]


def weight_kernel(slot_ref, slot_grad_ref, hidden_ref, pre_ref, w_in_ref, w_out_ref):
    w_out_ref[0] = tn(hidden_ref[0], slot_grad_ref[0]).astype(bf16)
    w_in_ref[0] = tn(slot_ref[0], pre_ref[0]).astype(bf16)


def second_sum_kernel(x_ref, in0, in1, in2, in3, slot_ref, lse_ref, out_ref):
    place = x_ref[0] // 2
    row = in0[...].astype(f32) + in1[...].astype(f32) + in2[...].astype(f32) + in3[...].astype(f32)
    row = row.astype(bf16).astype(f32)
    shift = jnp.sum(slot_ref[place].astype(f32) * row, axis=1, keepdims=True)
    columns = in_lanes((shift * 0.0,) * 3 + pieces(shift))
    write_rows(out_ref, row, lse_ref[place] + columns)


def token_kernel(
    core_ref, got_ref, logits_ref, tok_ref, grad_ref,
    slot_out_ref, in_half_ref, mix_ref, keep_ref, give_ref, sums,
):
    slots = logits_ref.shape[0]
    width = tok_ref.shape[1]
    owners = 16
    held = slots // owners
    lses, shifts = [], []
    for place in range(held):
        span = slice(place * owners, (place + 1) * owners)
        first, extra = read_rows(got_ref, place * 2, owners)
        second, _ = read_rows(got_ref, 4 + place * 2, owners)
        slot_out_ref[span] = (first + second).astype(bf16)
        lses.append(from_lanes(extra, 0))
        first, extra_a = read_rows(got_ref, place * 2 + 1, owners)
        second, extra_b = read_rows(got_ref, 4 + place * 2 + 1, owners)
        in_half_ref[span] = (first + second).astype(bf16)
        shifts.append(from_lanes(extra_a, 3) + from_lanes(extra_b, 3))
    lse = jnp.concatenate(lses, axis=0)
    shift = jnp.concatenate(shifts, axis=0)
    logits = logits_ref[...]
    probs = slot_softmax(logits)
    share = jnp.exp(logits - lse)
    grad_probs = nt(slot_out_ref[...], grad_ref[...])
    comb = probs * (grad_probs - jnp.sum(probs * grad_probs, axis=0, keepdims=True))
    inner = nt(in_half_ref[...], tok_ref[...])
    logit_grad = (comb + share * (inner - shift)).astype(bf16)
    mix_ref[0:slots] = probs.astype(bf16)
    mix_ref[slots : 2 * slots] = logit_grad
    mix_ref[2 * slots : 3 * slots] = share.astype(bf16)
    total = nn(logit_grad, tok_ref[...])
    half = slots // 2
    sums[0] = total[:half]
    sums[1] = total[half:]
    core = core_ref[0]
    keep_ref[...] = sums[core]
    give_ref[...] = sums[1 - core]


def router_split_kernel(keep_ref, got_ref, out_ref):
    width = keep_ref.shape[1]
    share = width // 8
    total = keep_ref[...] + got_ref[...]
    rest = jnp.zeros((keep_ref.shape[0], out_ref.shape[2] - share), bf16)
    for member in range(8):
        part = total[:, member * share : (member + 1) * share].astype(bf16)
        for copy in range(8):
            out_ref[member * 8 + copy, :, :share] = part
            out_ref[member * 8 + copy, :, share:] = rest


def router_sum_kernel(got_ref, out_ref):
    total = got_ref[0].astype(f32)
    for member in range(1, got_ref.shape[0]):
        total = total + got_ref[member].astype(f32)
    out_ref[...] = total


def mix_kernel(mix_ref, slot_out_ref, in_half_ref, router_ref, mixed_ref, grad_ref):
    slots, width = slot_out_ref.shape
    mixed_ref[...] = tn(mix_ref[0:slots], slot_out_ref[...]).astype(bf16)
    table = jnp.concatenate(
        [router_rows(router_ref, 16, slots // 16), in_half_ref[...]], axis=0
    )
    grad_ref[...] = tn(mix_ref[slots : 3 * slots], table).astype(bf16)


def around_x(arrays):
    got = [arrays[0]]
    for turn in range(1, 4):
        pairs = [(place, (place + turn) % 4) for place in range(4)]
        got.append(lax.ppermute(arrays[turn], "x", pairs))
    return got


def params(mib):
    return pltpu.CompilerParams(vmem_limit_bytes=mib * MIB)


def per_device(tokens, router, w_in, w_out, grad_out):
    x = lax.axis_index("x").astype(jnp.int32).reshape(1)
    core = lax.axis_index("core").astype(jnp.int32).reshape(1)
    tok = tokens[0]
    grad = grad_out[0]
    length, width = tok.shape
    slots = router.shape[1]
    held, _, units = w_in.shape
    owners = slots // held
    wide = width + LANES
    sent = shape((8 * owners, 2, width // 2 + LANES), bf16)
    token_flops = 2 * length * width * slots
    expert_flops = 2 * held * owners * width * units

    *send, logits = pl.pallas_call(
        first_kernel,
        out_shape=[shape((owners, wide), bf16)] * 4 + [shape((slots, length), f32)],
        in_specs=[SMEM, HBM, VMEM, HBM],
        out_specs=[VMEM] * 5,
        scratch_shapes=[
            pltpu.VMEM((length, width), bf16),
            pltpu.VMEM((length, width), bf16),
            pltpu.VMEM((4, owners, wide), bf16),
            pltpu.SemaphoreType.DMA((2 * CHUNKS,)),
        ],
        compiler_params=params(24),
        cost_estimate=cost(3 * token_flops, 4 * length * width),
        name="first",
    )(x, tok, router, grad)
    got = around_x(send)
    send = pl.pallas_call(
        first_sum_kernel,
        out_shape=sent,
        in_specs=[SMEM] + [VMEM] * 4,
        out_specs=VMEM,
        compiler_params=params(8),
        name="first_sum",
    )(x, *got)
    got = lax.all_to_all(send, ALL, 0, 0, tiled=True)
    *send, slot, slot_grad, hidden, pre, lse = pl.pallas_call(
        expert_kernel,
        out_shape=[shape((owners, width), bf16)] * 4
        + [shape((held, owners, width), bf16)] * 2
        + [shape((held, owners, units), bf16)] * 2
        + [shape((held, owners, LANES), f32)],
        in_specs=[SMEM] + [VMEM] * 3,
        out_specs=[VMEM] * 9,
        scratch_shapes=[pltpu.VMEM((4, owners, width), bf16)],
        compiler_params=params(24),
        cost_estimate=cost(4 * expert_flops, 4 * held * width * units),
        name="experts",
    )(x, got, w_in, w_out)
    got = around_x(send)
    send = pl.pallas_call(
        second_sum_kernel,
        out_shape=sent,
        in_specs=[SMEM] + [VMEM] * 6,
        out_specs=VMEM,
        compiler_params=params(8),
        name="second_sum",
    )(x, *got, slot, lse)
    got = lax.all_to_all(send, ALL, 0, 0, tiled=True)
    rows = lambda last: pl.BlockSpec((1, owners, last), lambda k: (k, 0, 0))
    grad_w_in, grad_w_out = pl.pallas_call(
        weight_kernel,
        grid=(held,),
        out_shape=[shape((held, width, units), bf16), shape((held, units, width), bf16)],
        in_specs=[rows(width), rows(width), rows(units), rows(units)],
        out_specs=[
            pl.BlockSpec((1, width, units), lambda k: (k, 0, 0)),
            pl.BlockSpec((1, units, width), lambda k: (k, 0, 0)),
        ],
        compiler_params=params(24),
        cost_estimate=cost(2 * expert_flops * 8, 4 * held * width * units),
        name="weights",
    )(slot, slot_grad, hidden, pre)
    slot_out, in_half, mix, keep, give = pl.pallas_call(
        token_kernel,
        out_shape=[shape((slots, width), bf16)] * 2
        + [shape((3 * slots, length), bf16)]
        + [shape((slots // 2, width), f32)] * 2,
        in_specs=[SMEM] + [VMEM] * 4,
        out_specs=[VMEM] * 5,
        scratch_shapes=[pltpu.VMEM((2, slots // 2, width), f32)],
        compiler_params=params(24),
        cost_estimate=cost(3 * token_flops, 4 * length * width),
        name="tokens",
    )(core, got, logits, tok, grad)
    swap = [(0, 1), (1, 0)]
    got = lax.ppermute(give, "core", swap)
    send = pl.pallas_call(
        router_split_kernel,
        out_shape=shape((64, slots // 2, 256), bf16),
        in_specs=[VMEM] * 2,
        out_specs=VMEM,
        compiler_params=params(8),
        name="router_split",
    )(keep, got)
    got = lax.all_to_all(send, CHIPS, 0, 0, tiled=True)
    half = pl.pallas_call(
        router_sum_kernel,
        out_shape=shape((slots // 2, 256), f32),
        in_specs=[VMEM],
        out_specs=VMEM,
        compiler_params=params(8),
        name="router_sum",
    )(got)
    other = lax.ppermute(half, "core", swap)
    chunk = length // 4
    mixed, grad_tokens = pl.pallas_call(
        mix_kernel,
        grid=(4,),
        out_shape=[shape((length, width), bf16)] * 2,
        in_specs=[
            pl.BlockSpec((3 * slots, chunk), lambda i: (0, i)),
            pl.BlockSpec((slots, width), lambda i: (0, 0)),
            pl.BlockSpec((slots, width), lambda i: (0, 0)),
            pl.BlockSpec((width, slots), lambda i: (0, 0)),
        ],
        out_specs=[pl.BlockSpec((chunk, width), lambda i: (i, 0))] * 2,
        compiler_params=params(24),
        cost_estimate=cost(3 * token_flops * 4, 4 * length * width),
        name="mix",
    )(mix, slot_out, in_half, router)
    share = width // 8
    first = jnp.where(core[0] == 0, half, other)
    second = jnp.where(core[0] == 0, other, half)
    grad_router = jnp.stack([first, second], axis=0)[:, :, :share]
    grad_router = grad_router.transpose(2, 1, 0).reshape(share, slots)
    return (mixed[None], grad_tokens[None], grad_router, grad_w_in, grad_w_out)


def solution(mesh):
    fine = Mesh(mesh.devices.reshape(2, 4, 4, 2, 2), ALL)
    in_specs = (
        P(EXP, SEQ, None),
        P(),
        P(EXP, None, SEQ),
        P(EXP, SEQ, None),
        P(EXP, SEQ, None),
    )
    out_specs = (
        P(EXP, SEQ, None),
        P(EXP, SEQ, None),
        P(SEQ, None),
        P(EXP, None, SEQ),
        P(EXP, SEQ, None),
    )
    return jax.shard_map(
        per_device, mesh=fine, in_specs=in_specs, out_specs=out_specs, check_vma=False
    )
```

```python
import math

import jax
import jax.numpy as jnp
from jax import lax
from jax.experimental import pallas as pl
from jax.experimental.pallas import tpu as pltpu
from jax.sharding import Mesh, PartitionSpec as P

bf16 = jnp.bfloat16
f32 = jnp.float32
ALL = ("yh", "x", "z", "yl", "core")
SEQ = ("yh", "x")
EXP = ("z", "yl", "core")
CHIPS = ("yh", "x", "z", "yl")
LANES = 128
CHUNKS = 4
MIB = 1024 * 1024

VMEM = pl.BlockSpec(memory_space=pltpu.VMEM)
SMEM = pl.BlockSpec(memory_space=pltpu.SMEM)
HBM = pl.BlockSpec(memory_space=pltpu.HBM)


def nn(a, b):
    return jnp.dot(a, b, preferred_element_type=f32)


def nt(a, b):
    return lax.dot_general(a, b, (((1,), (1,)), ((), ())), preferred_element_type=f32)


def tn(a, b):
    return lax.dot_general(a, b, (((0,), (0,)), ((), ())), preferred_element_type=f32)


def shape(dims, dtype):
    return jax.ShapeDtypeStruct(dims, dtype)


def cost(flops, moved):
    return pl.CostEstimate(flops=flops, bytes_accessed=moved, transcendentals=0)


def pieces(value):
    high = value.astype(bf16).astype(f32)
    rest = value - high
    middle = rest.astype(bf16).astype(f32)
    return high, middle, rest - middle


def in_lanes(columns):
    rows = columns[0].shape[0]
    lane = lax.broadcasted_iota(jnp.int32, (rows, LANES), 1)
    result = jnp.zeros((rows, LANES), f32)
    for place, column in enumerate(columns):
        result = jnp.where(lane == place, column, result)
    return result


def from_lanes(block, first):
    lane = lax.broadcasted_iota(jnp.int32, block.shape, 1)
    kept = jnp.where((lane >= first) & (lane < first + 3), block, 0.0)
    return jnp.sum(kept, axis=1, keepdims=True)


def log_sum_exp(values):
    top = values[0]
    for value in values[1:]:
        top = jnp.maximum(top, value)
    total = jnp.exp(values[0] - top)
    for value in values[1:]:
        total = total + jnp.exp(value - top)
    return top + jnp.log(total)


def normal(value):
    return 0.5 * (1.0 + lax.erf(value * (1.0 / math.sqrt(2.0))))


def slot_order(owners, held):
    slots = owners * held
    row = lax.broadcasted_iota(jnp.int32, (slots, slots), 0)
    column = lax.broadcasted_iota(jnp.int32, (slots, slots), 1)
    return (column == (row % owners) * held + row // owners).astype(bf16)


def router_rows(router_ref, owners, held):
    return nn(slot_order(owners, held), router_ref[...]).astype(bf16)


def fetches(sources, targets, sems):
    copies = []
    for source, target in zip(sources, targets):
        chunk = source.shape[0] // CHUNKS
        for part in range(CHUNKS):
            rows = pl.ds(part * chunk, chunk)
            copies.append(
                pltpu.make_async_copy(
                    source.at[rows, :], target.at[rows, :], sems.at[len(copies)]
                )
            )
    for copy in copies:
        copy.start()
    return copies


def slot_softmax(logits):
    top = jnp.max(logits, axis=0, keepdims=True)
    raw = jnp.exp(logits - top)
    return raw / jnp.sum(raw, axis=0, keepdims=True)


def first_kernel(
    place_ref, tok_ref, router_ref, grad_ref, out0, out1, out2, out3, logits_ref, tok, grad,
    held_rows, sems,
):
    length, width = tok_ref.shape
    slots = router_ref.shape[0]
    owners = out0.shape[0]
    held = slots // owners
    chunk = length // CHUNKS
    copies = fetches((tok_ref, grad_ref), (tok, grad), sems)
    table = router_rows(router_ref, owners, held)
    for part in range(CHUNKS):
        copies[part].wait()
        rows = pl.ds(part * chunk, chunk)
        logits_ref[:, rows] = nt(table, tok[rows, :])
    logits = logits_ref[...]
    top = jnp.max(logits, axis=1, keepdims=True)
    raw = jnp.exp(logits - top)
    total = jnp.sum(raw, axis=1, keepdims=True)
    local_slot = nn(raw.astype(bf16), tok[...]) / total
    lse = top + jnp.log(total)
    probs = slot_softmax(logits).astype(bf16)
    for copy in copies[CHUNKS:]:
        copy.wait()
    local_grad = nn(probs, grad[...])
    columns = []
    for place in range(held):
        columns += pieces(lse[place * owners : (place + 1) * owners])
    extra = in_lanes(columns).astype(bf16)
    for place in range(held):
        for array, value in enumerate((local_slot, local_grad)):
            quarter = place * 2 + array
            rows = value[place * owners : (place + 1) * owners]
            held_rows[quarter, :, :width] = rows.astype(bf16)
            held_rows[quarter, :, width:] = extra
    x = place_ref[0] % 4
    for turn, out in enumerate((out0, out1, out2, out3)):
        out[...] = held_rows[(x + turn) % 4]


def write_rows(out_ref, row, extra):
    owners, width = row.shape
    half = width // 2
    halves = [
        jnp.concatenate([row[:, :half], extra], axis=1),
        jnp.concatenate([row[:, half:], extra], axis=1),
    ]
    both = jnp.stack(halves, axis=1).astype(bf16)
    for member in range(out_ref.shape[0] // owners):
        out_ref[member * owners : (member + 1) * owners] = both


def read_rows(got_ref, member, owners):
    first = member * owners
    half = got_ref.shape[2] - LANES
    left = got_ref[first : first + owners, 0, :].astype(f32)
    right = got_ref[first : first + owners, 1, :].astype(f32)
    return jnp.concatenate([left[:, :half], right[:, :half]], axis=1), left[:, half:]


def first_sum_kernel(place_ref, in0, in1, in2, in3, out_ref):
    width = in0.shape[1] - LANES
    x = place_ref[0] % 4
    blocks = [ref[...].astype(f32) for ref in (in0, in1, in2, in3)]
    lses = []
    for block in blocks:
        extra = block[:, width:]
        lses.append(jnp.where(x // 2 == 0, from_lanes(extra, 0), from_lanes(extra, 3)))
    lse = log_sum_exp(lses)
    row = None
    for block, part in zip(blocks, lses):
        scale = jnp.where(x % 2 == 0, jnp.exp(part - lse), 1.0)
        term = block[:, :width] * scale
        row = term if row is None else row + term
    write_rows(out_ref, row, in_lanes(pieces(lse)))


def expert_kernel(
    place_ref, got_ref, w_in_ref, w_out_ref,
    out0, out1, out2, out3, own_slot_ref, own_lse_ref, rows_kept, units_kept,
    held_rows, held_lse,
):
    held = w_in_ref.shape[0]
    owners = out0.shape[0]
    for place in range(held):
        rows, lses = [], []
        for y in range(2):
            data, extra = read_rows(got_ref, y * 4 + place * 2, owners)
            rows.append(data)
            lses.append(from_lanes(extra, 0))
        lse = log_sum_exp(lses)
        slot = (
            rows[0] * jnp.exp(lses[0] - lse) + rows[1] * jnp.exp(lses[1] - lse)
        ).astype(bf16)
        grads = [read_rows(got_ref, y * 4 + place * 2 + 1, owners)[0] for y in range(2)]
        slot_grad = (grads[0] + grads[1]).astype(bf16)
        rows_kept[place * 2] = slot
        rows_kept[place * 2 + 1] = slot_grad
        held_lse[place] = in_lanes(pieces(lse))
        activation = nn(slot, w_in_ref[place])
        hidden_grad = nt(slot_grad, w_out_ref[place])
        cumulative = normal(activation)
        density = jnp.exp(-0.5 * activation * activation) * (1.0 / math.sqrt(2.0 * math.pi))
        hidden = (activation * cumulative).astype(bf16)
        pre = (hidden_grad * (cumulative + activation * density)).astype(bf16)
        units_kept[place * 2] = hidden
        units_kept[place * 2 + 1] = pre
        held_rows[place * 2] = nn(hidden, w_out_ref[place]).astype(bf16)
        held_rows[place * 2 + 1] = nt(pre, w_in_ref[place]).astype(bf16)
    x = place_ref[0] % 4
    for turn, out in enumerate((out0, out1, out2, out3)):
        out[...] = held_rows[(x + turn) % 4]
    own_slot_ref[...] = rows_kept[x // 2 * 2]
    own_lse_ref[...] = held_lse[x // 2]


def weight_kernel(rows_ref, units_ref, w_in_ref, w_out_ref):
    w_out_ref[0] = tn(units_ref[0], rows_ref[1]).astype(bf16)
    w_in_ref[0] = tn(rows_ref[0], units_ref[1]).astype(bf16)


def second_sum_kernel(in0, in1, in2, in3, slot_ref, lse_ref, out_ref):
    row = in0[...].astype(f32) + in1[...].astype(f32) + in2[...].astype(f32) + in3[...].astype(f32)
    row = row.astype(bf16).astype(f32)
    shift = jnp.sum(slot_ref[...].astype(f32) * row, axis=1, keepdims=True)
    columns = in_lanes((shift * 0.0,) * 3 + pieces(shift))
    write_rows(out_ref, row, lse_ref[...] + columns)


def token_kernel(
    place_ref, got_ref, logits_ref, tok_ref, grad_ref,
    mix, rows, keep_ref, give_ref, sums,
):
    slots, length = logits_ref.shape
    owners = 16
    held = slots // owners
    lses, shifts = [], []
    for place in range(held):
        first, extra = read_rows(got_ref, place * 2, owners)
        second, _ = read_rows(got_ref, 4 + place * 2, owners)
        rows[0, place * owners : (place + 1) * owners] = (first + second).astype(bf16)
        lses.append(from_lanes(extra, 0))
        first, extra_a = read_rows(got_ref, place * 2 + 1, owners)
        second, extra_b = read_rows(got_ref, 4 + place * 2 + 1, owners)
        rows[1, place * owners : (place + 1) * owners] = (first + second).astype(bf16)
        shifts.append(from_lanes(extra_a, 3) + from_lanes(extra_b, 3))
    lse = jnp.concatenate(lses, axis=0)
    shift = jnp.concatenate(shifts, axis=0)
    logits = logits_ref[...]
    probs = slot_softmax(logits)
    share = jnp.exp(logits - lse)
    mix[0] = probs.astype(bf16)
    mix[2] = share.astype(bf16)
    grad_probs = nt(rows[0], grad_ref[...])
    comb = probs * (grad_probs - jnp.sum(probs * grad_probs, axis=0, keepdims=True))
    inner = nt(rows[1], tok_ref[...])
    logit_grad = (comb + share * (inner - shift)).astype(bf16)
    mix[1] = logit_grad
    natural = tn(slot_order(owners, held), logit_grad).astype(bf16)
    total = nn(natural, tok_ref[...])
    half = slots // 2
    sums[0] = total[:half]
    sums[1] = total[half:]
    core = place_ref[0] // 4
    keep_ref[...] = sums[core]
    give_ref[...] = sums[1 - core]


def router_split_kernel(keep_ref, got_ref, out_ref):
    share = keep_ref.shape[1] // 8
    rows = out_ref.shape[1]
    total = keep_ref[...] + got_ref[...]
    for member in range(8):
        part = total[:, member * share : (member + 1) * share]
        packed = jnp.concatenate(
            [part[group * rows : (group + 1) * rows] for group in range(part.shape[0] // rows)],
            axis=1,
        ).astype(bf16)
        for copy in range(8):
            out_ref[member * 8 + copy] = packed


def router_sum_kernel(got_ref, out_ref):
    share = out_ref.shape[1]
    rows = got_ref.shape[1]
    total = got_ref[0].astype(f32)
    for member in range(1, got_ref.shape[0]):
        total = total + got_ref[member].astype(f32)
    for group in range(out_ref.shape[0] // rows):
        out_ref[group * rows : (group + 1) * rows] = total[:, group * share : (group + 1) * share]


def router_join_kernel(place_ref, half_ref, other_ref, out_ref):
    half = half_ref.shape[0]
    first = place_ref[0] // 4 == 0
    own, other = half_ref[...], other_ref[...]
    out_ref[:half] = jnp.where(first, own, other)
    out_ref[half:] = jnp.where(first, other, own)


def mix_kernel(mix_ref, rows_ref, router_ref, mixed_ref, grad_ref):
    slots = rows_ref.shape[1]
    mixed_ref[...] = tn(mix_ref[0], rows_ref[0]).astype(bf16)
    table = jnp.concatenate([router_rows(router_ref, 16, slots // 16), rows_ref[1]], axis=0)
    both = jnp.concatenate([mix_ref[1], mix_ref[2]], axis=0)
    grad_ref[...] = tn(both, table).astype(bf16)


def around_x(arrays):
    got = [arrays[0]]
    for turn in range(1, 4):
        pairs = [(place, (place + turn) % 4) for place in range(4)]
        got.append(lax.ppermute(arrays[turn], "x", pairs))
    return got


def params(mib):
    return pltpu.CompilerParams(vmem_limit_bytes=mib * MIB)


def per_device(tokens, router, w_in, w_out, grad_out):
    place = (lax.axis_index("x") + 4 * lax.axis_index("core")).astype(jnp.int32).reshape(1)
    tok = tokens[0]
    grad = grad_out[0]
    length, width = tok.shape
    router_t = router.T
    slots = router.shape[1]
    held, _, units = w_in.shape
    owners = slots // held
    wide = width + LANES
    sent = shape((8 * owners, 2, width // 2 + LANES), bf16)
    token_flops = 2 * length * width * slots
    expert_flops = 2 * held * owners * width * units

    *send, logits, tok_held, grad_held = pl.pallas_call(
        first_kernel,
        out_shape=[shape((owners, wide), bf16)] * 4
        + [shape((slots, length), f32)]
        + [shape((length, width), bf16)] * 2,
        in_specs=[SMEM, HBM, VMEM, HBM],
        out_specs=[VMEM] * 7,
        scratch_shapes=[
            pltpu.VMEM((4, owners, wide), bf16),
            pltpu.SemaphoreType.DMA((2 * CHUNKS,)),
        ],
        compiler_params=params(48),
        cost_estimate=cost(3 * token_flops, 4 * length * width),
        name="first",
    )(place, tok, router_t, grad)
    got = around_x(send)
    send = pl.pallas_call(
        first_sum_kernel,
        out_shape=sent,
        in_specs=[SMEM] + [VMEM] * 4,
        out_specs=VMEM,
        compiler_params=params(8),
        name="first_sum",
    )(place, *got)
    got = lax.all_to_all(send, ALL, 0, 0, tiled=True)
    *send, own_slot, own_lse, rows, units_held = pl.pallas_call(
        expert_kernel,
        out_shape=[shape((owners, width), bf16)] * 5
        + [shape((owners, LANES), f32)]
        + [shape((2 * held, owners, width), bf16), shape((2 * held, owners, units), bf16)],
        in_specs=[SMEM] + [VMEM] * 3,
        out_specs=[VMEM] * 8,
        scratch_shapes=[
            pltpu.VMEM((4, owners, width), bf16),
            pltpu.VMEM((held, owners, LANES), f32),
        ],
        compiler_params=params(8),
        cost_estimate=cost(4 * expert_flops, 4 * held * width * units),
        name="experts",
    )(place, got, w_in, w_out)
    got = around_x(send)
    send = pl.pallas_call(
        second_sum_kernel,
        out_shape=sent,
        in_specs=[VMEM] * 6,
        out_specs=VMEM,
        compiler_params=params(8),
        name="second_sum",
    )(*got, own_slot, own_lse)
    got = lax.all_to_all(send, ALL, 0, 0, tiled=True)
    mix, backs, keep, give = pl.pallas_call(
        token_kernel,
        out_shape=[shape((3, slots, length), bf16), shape((2, slots, width), bf16)]
        + [shape((slots // 2, width), f32)] * 2,
        in_specs=[SMEM] + [VMEM] * 4,
        out_specs=[VMEM] * 4,
        scratch_shapes=[pltpu.VMEM((2, slots // 2, width), f32)],
        compiler_params=params(8),
        cost_estimate=cost(3 * token_flops, 4 * length * width),
        name="tokens",
    )(place, got, logits, tok_held, grad_held)
    swap = [(0, 1), (1, 0)]
    got = lax.ppermute(give, "core", swap)
    share = width // 8
    send = pl.pallas_call(
        router_split_kernel,
        out_shape=shape((64, 4, 4 * share), bf16),
        in_specs=[VMEM] * 2,
        out_specs=VMEM,
        compiler_params=params(8),
        name="router_split",
    )(keep, got)
    send, rows, units_held, mix, backs = lax.optimization_barrier(
        (send, rows, units_held, mix, backs)
    )
    got = lax.all_to_all(send, CHIPS, 0, 0, tiled=True)
    grad_w_in, grad_w_out = pl.pallas_call(
        weight_kernel,
        grid=(held,),
        out_shape=[shape((held, width, units), bf16), shape((held, units, width), bf16)],
        in_specs=[
            pl.BlockSpec((2, owners, width), lambda k: (k, 0, 0)),
            pl.BlockSpec((2, owners, units), lambda k: (k, 0, 0)),
        ],
        out_specs=[
            pl.BlockSpec((1, width, units), lambda k: (k, 0, 0)),
            pl.BlockSpec((1, units, width), lambda k: (k, 0, 0)),
        ],
        compiler_params=params(8),
        cost_estimate=cost(150 * expert_flops, 4 * held * width * units),
        name="weights",
    )(rows, units_held)
    chunk = length // 4
    mixed, grad_tokens = pl.pallas_call(
        mix_kernel,
        grid=(4,),
        out_shape=[shape((length, width), bf16)] * 2,
        in_specs=[
            pl.BlockSpec((3, slots, chunk), lambda i: (0, 0, i)),
            pl.BlockSpec((2, slots, width), lambda i: (0, 0, 0)),
            pl.BlockSpec((slots, width), lambda i: (0, 0)),
        ],
        out_specs=[pl.BlockSpec((chunk, width), lambda i: (i, 0))] * 2,
        compiler_params=params(8),
        cost_estimate=cost(60 * token_flops, 4 * length * width),
        name="mix",
    )(mix, backs, router_t)
    got, mixed, grad_tokens, grad_w_in, grad_w_out = lax.optimization_barrier(
        (got, mixed, grad_tokens, grad_w_in, grad_w_out)
    )
    half = pl.pallas_call(
        router_sum_kernel,
        out_shape=shape((slots // 2, share), f32),
        in_specs=[VMEM],
        out_specs=VMEM,
        compiler_params=params(8),
        name="router_sum",
    )(got)
    other = lax.ppermute(half, "core", swap)
    grad_router = pl.pallas_call(
        router_join_kernel,
        out_shape=shape((slots, share), f32),
        in_specs=[SMEM] + [VMEM] * 2,
        out_specs=VMEM,
        compiler_params=params(8),
        name="router_join",
    )(place, half, other)
    return (mixed[None], grad_tokens[None], grad_router.T, grad_w_in, grad_w_out)


def solution(mesh):
    fine = Mesh(mesh.devices.reshape(2, 4, 4, 2, 2), ALL)
    in_specs = (
        P(EXP, SEQ, None),
        P(),
        P(EXP, None, SEQ),
        P(EXP, SEQ, None),
        P(EXP, SEQ, None),
    )
    out_specs = (
        P(EXP, SEQ, None),
        P(EXP, SEQ, None),
        P(SEQ, None),
        P(EXP, None, SEQ),
        P(EXP, SEQ, None),
    )
    return jax.shard_map(
        per_device, mesh=fine, in_specs=in_specs, out_specs=out_specs, check_vma=False
    )
```

```python
import math

import jax
import jax.numpy as jnp
from jax import lax
from jax.experimental import pallas as pl
from jax.experimental.pallas import tpu as pltpu
from jax.sharding import Mesh, PartitionSpec as P

bf16 = jnp.bfloat16
f32 = jnp.float32
ALL = ("yh", "x", "z", "yl", "core")
SEQ = ("yh", "x")
EXP = ("z", "yl", "core")
CHIPS = ("yh", "x", "z", "yl")
LANES = 128
CHUNKS = 2
MIX_CHUNKS = 2
MIB = 1024 * 1024

VMEM = pl.BlockSpec(memory_space=pltpu.VMEM)
SMEM = pl.BlockSpec(memory_space=pltpu.SMEM)
HBM = pl.BlockSpec(memory_space=pltpu.HBM)


def nn(a, b):
    return jnp.dot(a, b, preferred_element_type=f32)


def nt(a, b):
    return lax.dot_general(a, b, (((1,), (1,)), ((), ())), preferred_element_type=f32)


def tn(a, b):
    return lax.dot_general(a, b, (((0,), (0,)), ((), ())), preferred_element_type=f32)


def shape(dims, dtype):
    return jax.ShapeDtypeStruct(dims, dtype)


def cost(flops, moved):
    return pl.CostEstimate(flops=flops, bytes_accessed=moved, transcendentals=0)


def pieces(value):
    high = value.astype(bf16).astype(f32)
    rest = value - high
    middle = rest.astype(bf16).astype(f32)
    return high, middle, rest - middle


def in_lanes(columns):
    rows = columns[0].shape[0]
    lane = lax.broadcasted_iota(jnp.int32, (rows, LANES), 1)
    result = jnp.zeros((rows, LANES), f32)
    for place, column in enumerate(columns):
        result = jnp.where(lane == place, column, result)
    return result


def from_lanes(block, first):
    lane = lax.broadcasted_iota(jnp.int32, block.shape, 1)
    kept = jnp.where((lane >= first) & (lane < first + 3), block, 0.0)
    return jnp.sum(kept, axis=1, keepdims=True)


def log_sum_exp(values):
    top = values[0]
    for value in values[1:]:
        top = jnp.maximum(top, value)
    total = jnp.exp(values[0] - top)
    for value in values[1:]:
        total = total + jnp.exp(value - top)
    return top + jnp.log(total)


def normal(value):
    return 0.5 * (1.0 + lax.erf(value * (1.0 / math.sqrt(2.0))))


def slot_order(owners, held):
    slots = owners * held
    row = lax.broadcasted_iota(jnp.int32, (slots, slots), 0)
    column = lax.broadcasted_iota(jnp.int32, (slots, slots), 1)
    return (column == (row % owners) * held + row // owners).astype(bf16)


def router_rows(router_ref, owners, held):
    return nn(slot_order(owners, held), router_ref[...]).astype(bf16)


def fetches(sources, targets, sems):
    copies = []
    for source, target in zip(sources, targets):
        chunk = source.shape[0] // CHUNKS
        for part in range(CHUNKS):
            rows = pl.ds(part * chunk, chunk)
            copies.append(
                pltpu.make_async_copy(
                    source.at[rows, :], target.at[rows, :], sems.at[len(copies)]
                )
            )
    for copy in copies:
        copy.start()
    return copies


def slot_softmax(logits):
    top = jnp.max(logits, axis=0, keepdims=True)
    raw = jnp.exp(logits - top)
    return raw / jnp.sum(raw, axis=0, keepdims=True)


def first_kernel(
    place_ref, tok_ref, router_ref, grad_ref, out0, out1, out2, out3, logits_ref, tok, grad,
    held_rows, sems,
):
    length, width = tok_ref.shape
    slots = router_ref.shape[0]
    owners = out0.shape[0]
    held = slots // owners
    chunk = length // CHUNKS
    copies = fetches((tok_ref, grad_ref), (tok, grad), sems)
    table = router_rows(router_ref, owners, held)
    for part in range(CHUNKS):
        copies[part].wait()
        rows = pl.ds(part * chunk, chunk)
        logits_ref[:, rows] = nt(table, tok[rows, :])
    logits = logits_ref[...]
    top = jnp.max(logits, axis=1, keepdims=True)
    raw = jnp.exp(logits - top)
    total = jnp.sum(raw, axis=1, keepdims=True)
    local_slot = nn(raw.astype(bf16), tok[...]) / total
    lse = top + jnp.log(total)
    probs = slot_softmax(logits).astype(bf16)
    for copy in copies[CHUNKS:]:
        copy.wait()
    local_grad = nn(probs, grad[...])
    columns = []
    for place in range(held):
        columns += pieces(lse[place * owners : (place + 1) * owners])
    extra = in_lanes(columns).astype(bf16)
    for place in range(held):
        for array, value in enumerate((local_slot, local_grad)):
            quarter = place * 2 + array
            rows = value[place * owners : (place + 1) * owners]
            held_rows[quarter, :, :width] = rows.astype(bf16)
            held_rows[quarter, :, width:] = extra
    x = place_ref[0] % 4
    for turn, out in enumerate((out0, out1, out2, out3)):
        out[...] = held_rows[(x + turn) % 4]


def write_rows(out_ref, row, extra):
    owners, width = row.shape
    half = width // 2
    halves = [
        jnp.concatenate([row[:, :half], extra], axis=1),
        jnp.concatenate([row[:, half:], extra], axis=1),
    ]
    both = jnp.stack(halves, axis=1).astype(bf16)
    for member in range(out_ref.shape[0] // owners):
        out_ref[member * owners : (member + 1) * owners] = both


def read_rows(got_ref, member, owners):
    first = member * owners
    half = got_ref.shape[2] - LANES
    left = got_ref[first : first + owners, 0, :].astype(f32)
    right = got_ref[first : first + owners, 1, :].astype(f32)
    return jnp.concatenate([left[:, :half], right[:, :half]], axis=1), left[:, half:]


def first_sum_kernel(place_ref, in0, in1, in2, in3, out_ref):
    width = in0.shape[1] - LANES
    x = place_ref[0] % 4
    blocks = [ref[...].astype(f32) for ref in (in0, in1, in2, in3)]
    lses = []
    for block in blocks:
        extra = block[:, width:]
        lses.append(jnp.where(x // 2 == 0, from_lanes(extra, 0), from_lanes(extra, 3)))
    lse = log_sum_exp(lses)
    row = None
    for block, part in zip(blocks, lses):
        scale = jnp.where(x % 2 == 0, jnp.exp(part - lse), 1.0)
        term = block[:, :width] * scale
        row = term if row is None else row + term
    write_rows(out_ref, row, in_lanes(pieces(lse)))


def expert_kernel(
    place_ref, got_ref, w_in_ref, w_out_ref,
    out0, out1, out2, out3, own_slot_ref, own_lse_ref, rows_kept, units_kept,
    held_rows, held_lse,
):
    held = w_in_ref.shape[0]
    owners = out0.shape[0]
    for place in range(held):
        rows, lses = [], []
        for y in range(2):
            data, extra = read_rows(got_ref, y * 4 + place * 2, owners)
            rows.append(data)
            lses.append(from_lanes(extra, 0))
        lse = log_sum_exp(lses)
        slot = (
            rows[0] * jnp.exp(lses[0] - lse) + rows[1] * jnp.exp(lses[1] - lse)
        ).astype(bf16)
        grads = [read_rows(got_ref, y * 4 + place * 2 + 1, owners)[0] for y in range(2)]
        slot_grad = (grads[0] + grads[1]).astype(bf16)
        rows_kept[place * 2] = slot
        rows_kept[place * 2 + 1] = slot_grad
        held_lse[place] = in_lanes(pieces(lse))
        activation = nn(slot, w_in_ref[place])
        hidden_grad = nt(slot_grad, w_out_ref[place])
        cumulative = normal(activation)
        density = jnp.exp(-0.5 * activation * activation) * (1.0 / math.sqrt(2.0 * math.pi))
        hidden = (activation * cumulative).astype(bf16)
        pre = (hidden_grad * (cumulative + activation * density)).astype(bf16)
        units_kept[place * 2] = hidden
        units_kept[place * 2 + 1] = pre
        held_rows[place * 2] = nn(hidden, w_out_ref[place]).astype(bf16)
        held_rows[place * 2 + 1] = nt(pre, w_in_ref[place]).astype(bf16)
    x = place_ref[0] % 4
    for turn, out in enumerate((out0, out1, out2, out3)):
        out[...] = held_rows[(x + turn) % 4]
    own_slot_ref[...] = rows_kept[x // 2 * 2]
    own_lse_ref[...] = held_lse[x // 2]


def second_sum_kernel(in0, in1, in2, in3, slot_ref, lse_ref, out_ref):
    row = in0[...].astype(f32) + in1[...].astype(f32) + in2[...].astype(f32) + in3[...].astype(f32)
    row = row.astype(bf16).astype(f32)
    shift = jnp.sum(slot_ref[...].astype(f32) * row, axis=1, keepdims=True)
    columns = in_lanes((shift * 0.0,) * 3 + pieces(shift))
    write_rows(out_ref, row, lse_ref[...] + columns)


def token_kernel(
    place_ref, got_ref, logits_ref, tok_ref, grad_ref,
    mix, rows, keep_ref, give_ref, sums,
):
    slots, length = logits_ref.shape
    owners = 16
    held = slots // owners
    lses, shifts = [], []
    for place in range(held):
        first, extra = read_rows(got_ref, place * 2, owners)
        second, _ = read_rows(got_ref, 4 + place * 2, owners)
        rows[0, place * owners : (place + 1) * owners] = (first + second).astype(bf16)
        lses.append(from_lanes(extra, 0))
        first, extra_a = read_rows(got_ref, place * 2 + 1, owners)
        second, extra_b = read_rows(got_ref, 4 + place * 2 + 1, owners)
        rows[1, place * owners : (place + 1) * owners] = (first + second).astype(bf16)
        shifts.append(from_lanes(extra_a, 3) + from_lanes(extra_b, 3))
    lse = jnp.concatenate(lses, axis=0)
    shift = jnp.concatenate(shifts, axis=0)
    logits = logits_ref[...]
    probs = slot_softmax(logits)
    share = jnp.exp(logits - lse)
    mix[0] = probs.astype(bf16)
    mix[2] = share.astype(bf16)
    grad_probs = nt(rows[0], grad_ref[...])
    comb = probs * (grad_probs - jnp.sum(probs * grad_probs, axis=0, keepdims=True))
    inner = nt(rows[1], tok_ref[...])
    logit_grad = (comb + share * (inner - shift)).astype(bf16)
    mix[1] = logit_grad
    natural = tn(slot_order(owners, held), logit_grad).astype(bf16)
    total = nn(natural, tok_ref[...])
    half = slots // 2
    sums[0] = total[:half]
    sums[1] = total[half:]
    core = place_ref[0] // 4
    keep_ref[...] = sums[core]
    give_ref[...] = sums[1 - core]


def router_split_kernel(keep_ref, got_ref, out_ref):
    share = keep_ref.shape[1] // 8
    rows = out_ref.shape[1]
    total = keep_ref[...] + got_ref[...]
    for member in range(8):
        part = total[:, member * share : (member + 1) * share]
        packed = jnp.concatenate(
            [part[group * rows : (group + 1) * rows] for group in range(part.shape[0] // rows)],
            axis=1,
        ).astype(bf16)
        for copy in range(8):
            out_ref[member * 8 + copy] = packed


def router_sum_kernel(got_ref, out_ref):
    share = out_ref.shape[1]
    rows = got_ref.shape[1]
    total = got_ref[0].astype(f32)
    for member in range(1, got_ref.shape[0]):
        total = total + got_ref[member].astype(f32)
    for group in range(out_ref.shape[0] // rows):
        out_ref[group * rows : (group + 1) * rows] = total[:, group * share : (group + 1) * share]


def router_join_kernel(place_ref, half_ref, other_ref, out_ref):
    half = half_ref.shape[0]
    first = place_ref[0] // 4 == 0
    own, other = half_ref[...], other_ref[...]
    out_ref[:half] = jnp.where(first, own, other)
    out_ref[half:] = jnp.where(first, other, own)


def late_kernel(
    rows_ref, units_ref, mix_ref, back_ref, router_ref, w_in_ref, w_out_ref, mixed_ref, grad_ref,
    w_in, w_out, mixed, grad, sems, mix_sems,
):
    held, width, units = w_in.shape
    chunk = mixed.shape[0] // MIX_CHUNKS
    slots = back_ref.shape[1]

    def weight_copies(place):
        return [
            pltpu.make_async_copy(kept.at[place], ref.at[place], sems.at[2 * place + number])
            for number, (kept, ref) in enumerate(((w_out, w_out_ref), (w_in, w_in_ref)))
        ]

    def weight_step(place, carry):
        first, second = weight_copies(place)
        w_out[place] = tn(units_ref[place * 2], rows_ref[place * 2 + 1]).astype(bf16)
        first.start()
        w_in[place] = tn(rows_ref[place * 2], units_ref[place * 2 + 1]).astype(bf16)
        second.start()
        return carry

    def mix_copies(part):
        span = pl.ds(pl.multiple_of(part * chunk, chunk), chunk)
        return [
            pltpu.make_async_copy(kept.at[span, :], ref.at[span, :], mix_sems.at[2 * part + number])
            for number, (kept, ref) in enumerate(((mixed, mixed_ref), (grad, grad_ref)))
        ]

    def mix_step(part, carry):
        first, second = mix_copies(part)
        span = pl.ds(pl.multiple_of(part * chunk, chunk), chunk)
        mixed[span, :] = tn(mix_ref[0, :, span], back_ref[0]).astype(bf16)
        first.start()
        both = jnp.concatenate([mix_ref[1, :, span], mix_ref[2, :, span]], axis=0)
        grad[span, :] = tn(both, table).astype(bf16)
        second.start()
        return carry

    def wait(copies):
        def step(part, carry):
            for copy in copies(part):
                copy.wait()
            return carry

        return step

    table = jnp.concatenate([router_rows(router_ref, slots // held, held), back_ref[1]], axis=0)
    lax.fori_loop(0, held, weight_step, 0)
    lax.fori_loop(0, MIX_CHUNKS, mix_step, 0)
    lax.fori_loop(0, held, wait(weight_copies), 0)
    lax.fori_loop(0, MIX_CHUNKS, wait(mix_copies), 0)


def around_x(arrays):
    got = [arrays[0]]
    for turn in range(1, 4):
        pairs = [(place, (place + turn) % 4) for place in range(4)]
        got.append(lax.ppermute(arrays[turn], "x", pairs))
    return got


def params(mib):
    return pltpu.CompilerParams(vmem_limit_bytes=mib * MIB)


def per_device(tokens, router, w_in, w_out, grad_out):
    place = (lax.axis_index("x") + 4 * lax.axis_index("core")).astype(jnp.int32).reshape(1)
    tok = tokens[0]
    grad = grad_out[0]
    length, width = tok.shape
    router_t = router.T
    slots = router.shape[1]
    held, _, units = w_in.shape
    owners = slots // held
    wide = width + LANES
    sent = shape((8 * owners, 2, width // 2 + LANES), bf16)
    token_flops = 2 * length * width * slots
    expert_flops = 2 * held * owners * width * units

    *send, logits, tok_held, grad_held = pl.pallas_call(
        first_kernel,
        out_shape=[shape((owners, wide), bf16)] * 4
        + [shape((slots, length), f32)]
        + [shape((length, width), bf16)] * 2,
        in_specs=[SMEM, HBM, VMEM, HBM],
        out_specs=[VMEM] * 7,
        scratch_shapes=[
            pltpu.VMEM((4, owners, wide), bf16),
            pltpu.SemaphoreType.DMA((2 * CHUNKS,)),
        ],
        compiler_params=params(48),
        cost_estimate=cost(3 * token_flops, 4 * length * width),
        name="first",
    )(place, tok, router_t, grad)
    got = around_x(send)
    send = pl.pallas_call(
        first_sum_kernel,
        out_shape=sent,
        in_specs=[SMEM] + [VMEM] * 4,
        out_specs=VMEM,
        compiler_params=params(8),
        name="first_sum",
    )(place, *got)
    got = lax.all_to_all(send, ALL, 0, 0, tiled=True)
    *send, own_slot, own_lse, rows, units_held = pl.pallas_call(
        expert_kernel,
        out_shape=[shape((owners, width), bf16)] * 5
        + [shape((owners, LANES), f32)]
        + [shape((2 * held, owners, width), bf16), shape((2 * held, owners, units), bf16)],
        in_specs=[SMEM] + [VMEM] * 3,
        out_specs=[VMEM] * 8,
        scratch_shapes=[
            pltpu.VMEM((4, owners, width), bf16),
            pltpu.VMEM((held, owners, LANES), f32),
        ],
        compiler_params=params(8),
        cost_estimate=cost(4 * expert_flops, 4 * held * width * units),
        name="experts",
    )(place, got, w_in, w_out)
    got = around_x(send)
    send = pl.pallas_call(
        second_sum_kernel,
        out_shape=sent,
        in_specs=[VMEM] * 6,
        out_specs=VMEM,
        compiler_params=params(8),
        name="second_sum",
    )(*got, own_slot, own_lse)
    got = lax.all_to_all(send, ALL, 0, 0, tiled=True)
    mix, backs, keep, give = pl.pallas_call(
        token_kernel,
        out_shape=[shape((3, slots, length), bf16), shape((2, slots, width), bf16)]
        + [shape((slots // 2, width), f32)] * 2,
        in_specs=[SMEM] + [VMEM] * 4,
        out_specs=[VMEM] * 4,
        scratch_shapes=[pltpu.VMEM((2, slots // 2, width), f32)],
        compiler_params=params(8),
        cost_estimate=cost(3 * token_flops, 4 * length * width),
        name="tokens",
    )(place, got, logits, tok_held, grad_held)
    swap = [(0, 1), (1, 0)]
    got = lax.ppermute(give, "core", swap)
    share = width // 8
    send = pl.pallas_call(
        router_split_kernel,
        out_shape=shape((64, 4, 4 * share), bf16),
        in_specs=[VMEM] * 2,
        out_specs=VMEM,
        compiler_params=params(8),
        name="router_split",
    )(keep, got)
    send, rows, units_held, mix, backs = lax.optimization_barrier(
        (send, rows, units_held, mix, backs)
    )
    got = lax.all_to_all(send, CHIPS, 0, 0, tiled=True)
    late_shapes = [(held, width, units), (held, units, width), (length, width), (length, width)]
    grad_w_in, grad_w_out, mixed, grad_tokens = pl.pallas_call(
        late_kernel,
        out_shape=[shape(dims, bf16) for dims in late_shapes],
        in_specs=[VMEM] * 5,
        out_specs=[HBM] * 4,
        scratch_shapes=[pltpu.VMEM(dims, bf16) for dims in late_shapes]
        + [
            pltpu.SemaphoreType.DMA((2 * held,)),
            pltpu.SemaphoreType.DMA((2 * MIX_CHUNKS,)),
        ],
        compiler_params=params(20),
        cost_estimate=cost(200 * expert_flops, 4 * length * width),
        name="late",
    )(rows, units_held, mix, backs, router_t)
    got, mixed, grad_tokens, grad_w_in, grad_w_out = lax.optimization_barrier(
        (got, mixed, grad_tokens, grad_w_in, grad_w_out)
    )
    half = pl.pallas_call(
        router_sum_kernel,
        out_shape=shape((slots // 2, share), f32),
        in_specs=[VMEM],
        out_specs=VMEM,
        compiler_params=params(8),
        name="router_sum",
    )(got)
    other = lax.ppermute(half, "core", swap)
    grad_router = pl.pallas_call(
        router_join_kernel,
        out_shape=shape((slots, share), f32),
        in_specs=[SMEM] + [VMEM] * 2,
        out_specs=VMEM,
        compiler_params=params(8),
        name="router_join",
    )(place, half, other)
    return (mixed[None], grad_tokens[None], grad_router.T, grad_w_in, grad_w_out)


def solution(mesh):
    fine = Mesh(mesh.devices.reshape(2, 4, 4, 2, 2), ALL)
    in_specs = (
        P(EXP, SEQ, None),
        P(),
        P(EXP, None, SEQ),
        P(EXP, SEQ, None),
        P(EXP, SEQ, None),
    )
    out_specs = (
        P(EXP, SEQ, None),
        P(EXP, SEQ, None),
        P(SEQ, None),
        P(EXP, None, SEQ),
        P(EXP, SEQ, None),
    )
    return jax.shard_map(
        per_device, mesh=fine, in_specs=in_specs, out_specs=out_specs, check_vma=False
    )
```

```python
import math

import jax
import jax.numpy as jnp
from jax import lax
from jax.experimental import pallas as pl
from jax.experimental.pallas import tpu as pltpu
from jax.sharding import Mesh, PartitionSpec as P

bf16 = jnp.bfloat16
f32 = jnp.float32
ALL = ("yh", "x", "z", "yl", "core")
SEQ = ("yh", "x")
EXP = ("z", "yl", "core")
CHIPS = ("yh", "x", "z", "yl")
LANES = 128
CHUNKS = 2
MIX_CHUNKS = 2
MIB = 1024 * 1024

VMEM = pl.BlockSpec(memory_space=pltpu.VMEM)
SMEM = pl.BlockSpec(memory_space=pltpu.SMEM)
HBM = pl.BlockSpec(memory_space=pltpu.HBM)


def nn(a, b):
    return jnp.dot(a, b, preferred_element_type=f32)


def nt(a, b):
    return lax.dot_general(a, b, (((1,), (1,)), ((), ())), preferred_element_type=f32)


def tn(a, b):
    return lax.dot_general(a, b, (((0,), (0,)), ((), ())), preferred_element_type=f32)


def shape(dims, dtype):
    return jax.ShapeDtypeStruct(dims, dtype)


def cost(flops, moved):
    return pl.CostEstimate(flops=flops, bytes_accessed=moved, transcendentals=0)


def pieces(value):
    high = value.astype(bf16).astype(f32)
    rest = value - high
    middle = rest.astype(bf16).astype(f32)
    return high, middle, rest - middle


def in_lanes(columns):
    rows = columns[0].shape[0]
    lane = lax.broadcasted_iota(jnp.int32, (rows, LANES), 1)
    result = jnp.zeros((rows, LANES), f32)
    for place, column in enumerate(columns):
        result = jnp.where(lane == place, column, result)
    return result


def from_lanes(block, first):
    lane = lax.broadcasted_iota(jnp.int32, block.shape, 1)
    kept = jnp.where((lane >= first) & (lane < first + 3), block, 0.0)
    return jnp.sum(kept, axis=1, keepdims=True)


def log_sum_exp(values):
    top = values[0]
    for value in values[1:]:
        top = jnp.maximum(top, value)
    total = jnp.exp(values[0] - top)
    for value in values[1:]:
        total = total + jnp.exp(value - top)
    return top + jnp.log(total)


def normal(value):
    return 0.5 * (1.0 + lax.erf(value * (1.0 / math.sqrt(2.0))))


def slot_order(owners, held):
    slots = owners * held
    row = lax.broadcasted_iota(jnp.int32, (slots, slots), 0)
    column = lax.broadcasted_iota(jnp.int32, (slots, slots), 1)
    return (column == (row % owners) * held + row // owners).astype(bf16)


def router_rows(router_ref, owners, held):
    return nn(slot_order(owners, held), router_ref[...]).astype(bf16)


def fetches(sources, targets, sems):
    copies = []
    for source, target in zip(sources, targets):
        chunk = source.shape[0] // CHUNKS
        for part in range(CHUNKS):
            rows = pl.ds(part * chunk, chunk)
            copies.append(
                pltpu.make_async_copy(
                    source.at[rows, :], target.at[rows, :], sems.at[len(copies)]
                )
            )
    for copy in copies:
        copy.start()
    return copies


def slot_softmax(logits):
    top = jnp.max(logits, axis=0, keepdims=True)
    raw = jnp.exp(logits - top)
    return raw / jnp.sum(raw, axis=0, keepdims=True)


def first_kernel(
    place_ref, tok_ref, router_ref, grad_ref, out0, out1, out2, out3, logits_ref, tok, grad,
    held_rows, sems,
):
    length, width = tok_ref.shape
    slots = router_ref.shape[0]
    owners = out0.shape[0]
    held = slots // owners
    chunk = length // CHUNKS
    copies = fetches((tok_ref, grad_ref), (tok, grad), sems)
    table = router_rows(router_ref, owners, held)
    for part in range(CHUNKS):
        copies[part].wait()
        rows = pl.ds(part * chunk, chunk)
        logits_ref[:, rows] = nt(table, tok[rows, :])
    logits = logits_ref[...]
    top = jnp.max(logits, axis=1, keepdims=True)
    raw = jnp.exp(logits - top)
    total = jnp.sum(raw, axis=1, keepdims=True)
    local_slot = nn(raw.astype(bf16), tok[...]) / total
    lse = top + jnp.log(total)
    probs = slot_softmax(logits).astype(bf16)
    for copy in copies[CHUNKS:]:
        copy.wait()
    local_grad = nn(probs, grad[...])
    columns = []
    for place in range(held):
        columns += pieces(lse[place * owners : (place + 1) * owners])
    extra = in_lanes(columns)
    for place in range(held):
        for array, value in enumerate((local_slot, local_grad)):
            quarter = place * 2 + array
            rows = value[place * owners : (place + 1) * owners]
            held_rows[quarter, :, :width] = rows
            held_rows[quarter, :, width:] = extra
    x = place_ref[0] % 4
    for turn, out in enumerate((out0, out1, out2, out3)):
        out[...] = held_rows[(x + turn) % 4]


def write_rows(out_ref, row, extra):
    owners, width = row.shape
    half = width // 2
    halves = [
        jnp.concatenate([row[:, :half], extra], axis=1),
        jnp.concatenate([row[:, half:], extra], axis=1),
    ]
    both = jnp.stack(halves, axis=1).astype(bf16)
    for member in range(out_ref.shape[0] // owners):
        out_ref[member * owners : (member + 1) * owners] = both


def read_rows(got_ref, member, owners):
    first = member * owners
    half = got_ref.shape[2] - LANES
    left = got_ref[first : first + owners, 0, :].astype(f32)
    right = got_ref[first : first + owners, 1, :].astype(f32)
    return jnp.concatenate([left[:, :half], right[:, :half]], axis=1), left[:, half:]


def first_sum_kernel(place_ref, in0, in1, in2, in3, out_ref):
    width = in0.shape[1] - LANES
    x = place_ref[0] % 4
    blocks = [ref[...].astype(f32) for ref in (in0, in1, in2, in3)]
    lses = []
    for block in blocks:
        extra = block[:, width:]
        lses.append(jnp.where(x // 2 == 0, from_lanes(extra, 0), from_lanes(extra, 3)))
    lse = log_sum_exp(lses)
    row = None
    for block, part in zip(blocks, lses):
        scale = jnp.where(x % 2 == 0, jnp.exp(part - lse), 1.0)
        term = block[:, :width] * scale
        row = term if row is None else row + term
    write_rows(out_ref, row, in_lanes(pieces(lse)))


def expert_kernel(
    place_ref, got_ref, w_in_ref, w_out_ref,
    out0, out1, out2, out3, own_slot_ref, own_lse_ref, rows_kept, units_kept,
    held_rows, held_lse, held_slots,
):
    held = w_in_ref.shape[0]
    owners = out0.shape[0]
    for place in range(held):
        rows, lses = [], []
        for y in range(2):
            data, extra = read_rows(got_ref, y * 4 + place * 2, owners)
            rows.append(data)
            lses.append(from_lanes(extra, 0))
        lse = log_sum_exp(lses)
        slot_full = rows[0] * jnp.exp(lses[0] - lse) + rows[1] * jnp.exp(lses[1] - lse)
        held_slots[place] = slot_full
        slot = slot_full.astype(bf16)
        grads = [read_rows(got_ref, y * 4 + place * 2 + 1, owners)[0] for y in range(2)]
        slot_grad = (grads[0] + grads[1]).astype(bf16)
        rows_kept[place * 2] = slot
        rows_kept[place * 2 + 1] = slot_grad
        held_lse[place] = in_lanes(pieces(lse))
        activation = nn(slot, w_in_ref[place])
        hidden_grad = nt(slot_grad, w_out_ref[place])
        cumulative = normal(activation)
        density = jnp.exp(-0.5 * activation * activation) * (1.0 / math.sqrt(2.0 * math.pi))
        hidden = (activation * cumulative).astype(bf16)
        pre = (hidden_grad * (cumulative + activation * density)).astype(bf16)
        units_kept[place * 2] = hidden
        units_kept[place * 2 + 1] = pre
        held_rows[place * 2] = nn(hidden, w_out_ref[place]).astype(bf16)
        held_rows[place * 2 + 1] = nt(pre, w_in_ref[place]).astype(bf16)
    x = place_ref[0] % 4
    for turn, out in enumerate((out0, out1, out2, out3)):
        out[...] = held_rows[(x + turn) % 4]
    own_slot_ref[...] = held_slots[x // 2]
    own_lse_ref[...] = held_lse[x // 2]


def second_sum_kernel(in0, in1, in2, in3, slot_ref, lse_ref, out_ref):
    row = in0[...].astype(f32) + in1[...].astype(f32) + in2[...].astype(f32) + in3[...].astype(f32)
    row = row.astype(bf16).astype(f32)
    shift = jnp.sum(slot_ref[...].astype(f32) * row, axis=1, keepdims=True)
    columns = in_lanes((shift * 0.0,) * 3 + pieces(shift))
    write_rows(out_ref, row, lse_ref[...] + columns)


def token_kernel(
    place_ref, got_ref, logits_ref, tok_ref, grad_ref,
    mix, rows, keep_ref, give_ref, halves, sums,
):
    slots, length = logits_ref.shape
    owners = 16
    held = slots // owners
    lses, shifts = [], []
    for place in range(held):
        first, extra = read_rows(got_ref, place * 2, owners)
        second, _ = read_rows(got_ref, 4 + place * 2, owners)
        rows[0, place * owners : (place + 1) * owners] = (first + second).astype(bf16)
        lses.append(from_lanes(extra, 0))
        first, extra_a = read_rows(got_ref, place * 2 + 1, owners)
        second, extra_b = read_rows(got_ref, 4 + place * 2 + 1, owners)
        rows[1, place * owners : (place + 1) * owners] = (first + second).astype(bf16)
        halves[place * owners : (place + 1) * owners] = first.astype(bf16)
        halves[slots + place * owners : slots + (place + 1) * owners] = second.astype(bf16)
        shifts.append(from_lanes(extra_a, 3) + from_lanes(extra_b, 3))
    lse = jnp.concatenate(lses, axis=0)
    shift = jnp.concatenate(shifts, axis=0)
    logits = logits_ref[...]
    probs = slot_softmax(logits)
    share = jnp.exp(logits - lse)
    mix[0] = probs.astype(bf16)
    mix[2] = share.astype(bf16)
    grad_probs = nt(rows[0], grad_ref[...])
    comb = probs * (grad_probs - jnp.sum(probs * grad_probs, axis=0, keepdims=True))
    inner = nt(halves[...], tok_ref[...])
    inner = inner[:slots] + inner[slots:]
    logit_grad = (comb + share * (inner - shift)).astype(bf16)
    mix[1] = logit_grad
    natural = tn(slot_order(owners, held), logit_grad).astype(bf16)
    total = nn(natural, tok_ref[...])
    half = slots // 2
    sums[0] = total[:half]
    sums[1] = total[half:]
    core = place_ref[0] // 4
    keep_ref[...] = sums[core]
    give_ref[...] = sums[1 - core]


def router_split_kernel(keep_ref, got_ref, out_ref):
    share = keep_ref.shape[1] // 8
    rows = out_ref.shape[1]
    total = keep_ref[...] + got_ref[...]
    for member in range(8):
        part = total[:, member * share : (member + 1) * share]
        packed = jnp.concatenate(
            [part[group * rows : (group + 1) * rows] for group in range(part.shape[0] // rows)],
            axis=1,
        ).astype(bf16)
        for copy in range(8):
            out_ref[member * 8 + copy] = packed


def router_sum_kernel(got_ref, out_ref):
    share = out_ref.shape[1]
    rows = got_ref.shape[1]
    total = got_ref[0].astype(f32)
    for member in range(1, got_ref.shape[0]):
        total = total + got_ref[member].astype(f32)
    for group in range(out_ref.shape[0] // rows):
        out_ref[group * rows : (group + 1) * rows] = total[:, group * share : (group + 1) * share]


def router_join_kernel(place_ref, half_ref, other_ref, out_ref):
    half = half_ref.shape[0]
    first = place_ref[0] // 4 == 0
    own, other = half_ref[...], other_ref[...]
    out_ref[:half] = jnp.where(first, own, other)
    out_ref[half:] = jnp.where(first, other, own)


def late_kernel(
    rows_ref, units_ref, mix_ref, back_ref, router_ref, w_in_ref, w_out_ref, mixed_ref, grad_ref,
    w_in, w_out, mixed, grad, sems, mix_sems,
):
    held, width, units = w_in.shape
    chunk = mixed.shape[0] // MIX_CHUNKS
    slots = back_ref.shape[1]

    def weight_copies(place):
        return [
            pltpu.make_async_copy(kept.at[place], ref.at[place], sems.at[2 * place + number])
            for number, (kept, ref) in enumerate(((w_out, w_out_ref), (w_in, w_in_ref)))
        ]

    def weight_step(place, carry):
        first, second = weight_copies(place)
        w_out[place] = tn(units_ref[place * 2], rows_ref[place * 2 + 1]).astype(bf16)
        first.start()
        w_in[place] = tn(rows_ref[place * 2], units_ref[place * 2 + 1]).astype(bf16)
        second.start()
        return carry

    def mix_copies(part):
        span = pl.ds(pl.multiple_of(part * chunk, chunk), chunk)
        return [
            pltpu.make_async_copy(kept.at[span, :], ref.at[span, :], mix_sems.at[2 * part + number])
            for number, (kept, ref) in enumerate(((mixed, mixed_ref), (grad, grad_ref)))
        ]

    def mix_step(part, carry):
        first, second = mix_copies(part)
        span = pl.ds(pl.multiple_of(part * chunk, chunk), chunk)
        mixed[span, :] = tn(mix_ref[0, :, span], back_ref[0]).astype(bf16)
        first.start()
        both = jnp.concatenate([mix_ref[1, :, span], mix_ref[2, :, span]], axis=0)
        grad[span, :] = tn(both, table).astype(bf16)
        second.start()
        return carry

    def wait(copies):
        def step(part, carry):
            for copy in copies(part):
                copy.wait()
            return carry

        return step

    table = jnp.concatenate([router_rows(router_ref, slots // held, held), back_ref[1]], axis=0)
    lax.fori_loop(0, held, weight_step, 0)
    lax.fori_loop(0, MIX_CHUNKS, mix_step, 0)
    lax.fori_loop(0, held, wait(weight_copies), 0)
    lax.fori_loop(0, MIX_CHUNKS, wait(mix_copies), 0)


def around_x(arrays):
    got = [arrays[0]]
    for turn in range(1, 4):
        pairs = [(place, (place + turn) % 4) for place in range(4)]
        got.append(lax.ppermute(arrays[turn], "x", pairs))
    return got


def params(mib):
    return pltpu.CompilerParams(vmem_limit_bytes=mib * MIB)


def per_device(tokens, router, w_in, w_out, grad_out):
    place = (lax.axis_index("x") + 4 * lax.axis_index("core")).astype(jnp.int32).reshape(1)
    tok = tokens[0]
    grad = grad_out[0]
    length, width = tok.shape
    router_t = router.T
    slots = router.shape[1]
    held, _, units = w_in.shape
    owners = slots // held
    wide = width + LANES
    sent = shape((8 * owners, 2, width // 2 + LANES), bf16)
    token_flops = 2 * length * width * slots
    expert_flops = 2 * held * owners * width * units

    *send, logits, tok_held, grad_held = pl.pallas_call(
        first_kernel,
        out_shape=[shape((owners, wide), f32)] * 4
        + [shape((slots, length), f32)]
        + [shape((length, width), bf16)] * 2,
        in_specs=[SMEM, HBM, VMEM, HBM],
        out_specs=[VMEM] * 7,
        scratch_shapes=[
            pltpu.VMEM((4, owners, wide), f32),
            pltpu.SemaphoreType.DMA((2 * CHUNKS,)),
        ],
        compiler_params=params(48),
        cost_estimate=cost(3 * token_flops, 4 * length * width),
        name="first",
    )(place, tok, router_t, grad)
    got = around_x(send)
    send = pl.pallas_call(
        first_sum_kernel,
        out_shape=sent,
        in_specs=[SMEM] + [VMEM] * 4,
        out_specs=VMEM,
        compiler_params=params(8),
        name="first_sum",
    )(place, *got)
    got = lax.all_to_all(send, ALL, 0, 0, tiled=True)
    *send, own_slot, own_lse, rows, units_held = pl.pallas_call(
        expert_kernel,
        out_shape=[shape((owners, width), bf16)] * 4
        + [shape((owners, width), f32), shape((owners, LANES), f32)]
        + [shape((2 * held, owners, width), bf16), shape((2 * held, owners, units), bf16)],
        in_specs=[SMEM] + [VMEM] * 3,
        out_specs=[VMEM] * 8,
        scratch_shapes=[
            pltpu.VMEM((4, owners, width), bf16),
            pltpu.VMEM((held, owners, LANES), f32),
            pltpu.VMEM((held, owners, width), f32),
        ],
        compiler_params=params(8),
        cost_estimate=cost(4 * expert_flops, 4 * held * width * units),
        name="experts",
    )(place, got, w_in, w_out)
    got = around_x(send)
    send = pl.pallas_call(
        second_sum_kernel,
        out_shape=sent,
        in_specs=[VMEM] * 6,
        out_specs=VMEM,
        compiler_params=params(8),
        name="second_sum",
    )(*got, own_slot, own_lse)
    got = lax.all_to_all(send, ALL, 0, 0, tiled=True)
    mix, backs, keep, give = pl.pallas_call(
        token_kernel,
        out_shape=[shape((3, slots, length), bf16), shape((2, slots, width), bf16)]
        + [shape((slots // 2, width), f32)] * 2,
        in_specs=[SMEM] + [VMEM] * 4,
        out_specs=[VMEM] * 4,
        scratch_shapes=[
            pltpu.VMEM((2 * slots, width), bf16),
            pltpu.VMEM((2, slots // 2, width), f32),
        ],
        compiler_params=params(8),
        cost_estimate=cost(3 * token_flops, 4 * length * width),
        name="tokens",
    )(place, got, logits, tok_held, grad_held)
    swap = [(0, 1), (1, 0)]
    got = lax.ppermute(give, "core", swap)
    share = width // 8
    send = pl.pallas_call(
        router_split_kernel,
        out_shape=shape((64, 4, 4 * share), bf16),
        in_specs=[VMEM] * 2,
        out_specs=VMEM,
        compiler_params=params(8),
        name="router_split",
    )(keep, got)
    send, rows, units_held, mix, backs = lax.optimization_barrier(
        (send, rows, units_held, mix, backs)
    )
    got = lax.all_to_all(send, CHIPS, 0, 0, tiled=True)
    late_shapes = [(held, width, units), (held, units, width), (length, width), (length, width)]
    grad_w_in, grad_w_out, mixed, grad_tokens = pl.pallas_call(
        late_kernel,
        out_shape=[shape(dims, bf16) for dims in late_shapes],
        in_specs=[VMEM] * 5,
        out_specs=[HBM] * 4,
        scratch_shapes=[pltpu.VMEM(dims, bf16) for dims in late_shapes]
        + [
            pltpu.SemaphoreType.DMA((2 * held,)),
            pltpu.SemaphoreType.DMA((2 * MIX_CHUNKS,)),
        ],
        compiler_params=params(20),
        cost_estimate=cost(200 * expert_flops, 4 * length * width),
        name="late",
    )(rows, units_held, mix, backs, router_t)
    got, mixed, grad_tokens, grad_w_in, grad_w_out = lax.optimization_barrier(
        (got, mixed, grad_tokens, grad_w_in, grad_w_out)
    )
    half = pl.pallas_call(
        router_sum_kernel,
        out_shape=shape((slots // 2, share), f32),
        in_specs=[VMEM],
        out_specs=VMEM,
        compiler_params=params(8),
        name="router_sum",
    )(got)
    other = lax.ppermute(half, "core", swap)
    grad_router = pl.pallas_call(
        router_join_kernel,
        out_shape=shape((slots, share), f32),
        in_specs=[SMEM] + [VMEM] * 2,
        out_specs=VMEM,
        compiler_params=params(8),
        name="router_join",
    )(place, half, other)
    return (mixed[None], grad_tokens[None], grad_router.T, grad_w_in, grad_w_out)


def solution(mesh):
    fine = Mesh(mesh.devices.reshape(2, 4, 4, 2, 2), ALL)
    in_specs = (
        P(EXP, SEQ, None),
        P(),
        P(EXP, None, SEQ),
        P(EXP, SEQ, None),
        P(EXP, SEQ, None),
    )
    out_specs = (
        P(EXP, SEQ, None),
        P(EXP, SEQ, None),
        P(SEQ, None),
        P(EXP, None, SEQ),
        P(EXP, SEQ, None),
    )
    return jax.shard_map(
        per_device, mesh=fine, in_specs=in_specs, out_specs=out_specs, check_vma=False
    )
```

```python
import math

import jax
import jax.numpy as jnp
from jax import lax
from jax.experimental import pallas as pl
from jax.experimental.pallas import tpu as pltpu
from jax.sharding import Mesh, PartitionSpec as P

bf16 = jnp.bfloat16
f32 = jnp.float32
ALL = ("yh", "x", "z", "yl", "core")
SEQ = ("yh", "x")
EXP = ("z", "yl", "core")
CHIPS = ("yh", "x", "z", "yl")
LANES = 128
CHUNKS = 2
MIX_CHUNKS = 2
MIB = 1024 * 1024

VMEM = pl.BlockSpec(memory_space=pltpu.VMEM)
SMEM = pl.BlockSpec(memory_space=pltpu.SMEM)
HBM = pl.BlockSpec(memory_space=pltpu.HBM)


def nn(a, b):
    return jnp.dot(a, b, preferred_element_type=f32)


def nt(a, b):
    return lax.dot_general(a, b, (((1,), (1,)), ((), ())), preferred_element_type=f32)


def tn(a, b):
    return lax.dot_general(a, b, (((0,), (0,)), ((), ())), preferred_element_type=f32)


def shape(dims, dtype):
    return jax.ShapeDtypeStruct(dims, dtype)


def cost(flops, moved):
    return pl.CostEstimate(flops=flops, bytes_accessed=moved, transcendentals=0)


def pieces(value):
    high = value.astype(bf16).astype(f32)
    rest = value - high
    middle = rest.astype(bf16).astype(f32)
    return high, middle, rest - middle


def in_lanes(columns):
    rows = columns[0].shape[0]
    lane = lax.broadcasted_iota(jnp.int32, (rows, LANES), 1)
    result = jnp.zeros((rows, LANES), f32)
    for place, column in enumerate(columns):
        result = jnp.where(lane == place, column, result)
    return result


def from_lanes(block, first):
    lane = lax.broadcasted_iota(jnp.int32, block.shape, 1)
    kept = jnp.where((lane >= first) & (lane < first + 3), block, 0.0)
    return jnp.sum(kept, axis=1, keepdims=True)


def log_sum_exp(values):
    top = values[0]
    for value in values[1:]:
        top = jnp.maximum(top, value)
    total = jnp.exp(values[0] - top)
    for value in values[1:]:
        total = total + jnp.exp(value - top)
    return top + jnp.log(total)


def normal(value):
    return 0.5 * (1.0 + lax.erf(value * (1.0 / math.sqrt(2.0))))


def slot_order(owners, held):
    slots = owners * held
    row = lax.broadcasted_iota(jnp.int32, (slots, slots), 0)
    column = lax.broadcasted_iota(jnp.int32, (slots, slots), 1)
    return (column == (row % owners) * held + row // owners).astype(bf16)


def router_rows(router_ref, owners, held):
    return nn(slot_order(owners, held), router_ref[...]).astype(bf16)


def fetches(sources, targets, sems):
    copies = []
    for source, target in zip(sources, targets):
        chunk = source.shape[0] // CHUNKS
        for part in range(CHUNKS):
            rows = pl.ds(part * chunk, chunk)
            copies.append(
                pltpu.make_async_copy(
                    source.at[rows, :], target.at[rows, :], sems.at[len(copies)]
                )
            )
    for copy in copies:
        copy.start()
    return copies


def slot_softmax(logits):
    top = jnp.max(logits, axis=0, keepdims=True)
    raw = jnp.exp(logits - top)
    return raw / jnp.sum(raw, axis=0, keepdims=True)


def first_kernel(
    place_ref, tok_ref, router_ref, grad_ref, out0, out1, out2, out3, logits_ref, tok, grad,
    held_rows, sems,
):
    length, width = tok_ref.shape
    slots = router_ref.shape[0]
    owners = out0.shape[0]
    held = slots // owners
    chunk = length // CHUNKS
    copies = fetches((tok_ref, grad_ref), (tok, grad), sems)
    table = router_rows(router_ref, owners, held)
    for part in range(CHUNKS):
        copies[part].wait()
        rows = pl.ds(part * chunk, chunk)
        logits_ref[:, rows] = nt(table, tok[rows, :])
    logits = logits_ref[...]
    top = jnp.max(logits, axis=1, keepdims=True)
    raw = jnp.exp(logits - top)
    total = jnp.sum(raw, axis=1, keepdims=True)
    local_slot = nn(raw.astype(bf16), tok[...]) / total
    lse = top + jnp.log(total)
    probs = slot_softmax(logits).astype(bf16)
    for copy in copies[CHUNKS:]:
        copy.wait()
    local_grad = nn(probs, grad[...])
    columns = []
    for place in range(held):
        columns += pieces(lse[place * owners : (place + 1) * owners])
    extra = in_lanes(columns)
    for place in range(held):
        for array, value in enumerate((local_slot, local_grad)):
            quarter = place * 2 + array
            rows = value[place * owners : (place + 1) * owners]
            held_rows[quarter, :, :width] = rows
            held_rows[quarter, :, width:] = extra
    x = place_ref[0] % 4
    for turn, out in enumerate((out0, out1, out2, out3)):
        out[...] = held_rows[(x + turn) % 4]


def write_rows(out_ref, row, extra):
    owners, width = row.shape
    half = width // 2
    halves = [
        jnp.concatenate([row[:, :half], extra], axis=1),
        jnp.concatenate([row[:, half:], extra], axis=1),
    ]
    both = jnp.stack(halves, axis=1).astype(out_ref.dtype)
    for member in range(out_ref.shape[0] // owners):
        out_ref[member * owners : (member + 1) * owners] = both


def read_rows(got_ref, member, owners):
    first = member * owners
    half = got_ref.shape[2] - LANES
    left = got_ref[first : first + owners, 0, :].astype(f32)
    right = got_ref[first : first + owners, 1, :].astype(f32)
    return jnp.concatenate([left[:, :half], right[:, :half]], axis=1), left[:, half:]


def first_sum_kernel(place_ref, in0, in1, in2, in3, out_ref):
    width = in0.shape[1] - LANES
    x = place_ref[0] % 4
    blocks = [ref[...].astype(f32) for ref in (in0, in1, in2, in3)]
    lses = []
    for block in blocks:
        extra = block[:, width:]
        lses.append(jnp.where(x // 2 == 0, from_lanes(extra, 0), from_lanes(extra, 3)))
    lse = log_sum_exp(lses)
    row = None
    for block, part in zip(blocks, lses):
        scale = jnp.where(x % 2 == 0, jnp.exp(part - lse), 1.0)
        term = block[:, :width] * scale
        row = term if row is None else row + term
    write_rows(out_ref, row, in_lanes(pieces(lse)))


def expert_kernel(
    place_ref, got_ref, w_in_ref, w_out_ref,
    out0, out1, out2, out3, own_slot_ref, own_lse_ref, rows_kept, units_kept,
    held_rows, held_lse, held_slots,
):
    held = w_in_ref.shape[0]
    owners = out0.shape[0]
    for place in range(held):
        rows, lses = [], []
        for y in range(2):
            data, extra = read_rows(got_ref, y * 4 + place * 2, owners)
            rows.append(data)
            lses.append(from_lanes(extra, 0))
        lse = log_sum_exp(lses)
        slot_full = rows[0] * jnp.exp(lses[0] - lse) + rows[1] * jnp.exp(lses[1] - lse)
        held_slots[place] = slot_full
        slot = slot_full.astype(bf16)
        grads = [read_rows(got_ref, y * 4 + place * 2 + 1, owners)[0] for y in range(2)]
        slot_grad = (grads[0] + grads[1]).astype(bf16)
        rows_kept[place * 2] = slot
        rows_kept[place * 2 + 1] = slot_grad
        held_lse[place] = in_lanes(pieces(lse))
        activation = nn(slot, w_in_ref[place])
        hidden_grad = nt(slot_grad, w_out_ref[place])
        cumulative = normal(activation)
        density = jnp.exp(-0.5 * activation * activation) * (1.0 / math.sqrt(2.0 * math.pi))
        hidden = (activation * cumulative).astype(bf16)
        pre = (hidden_grad * (cumulative + activation * density)).astype(bf16)
        units_kept[place * 2] = hidden
        units_kept[place * 2 + 1] = pre
        held_rows[place * 2] = nn(hidden, w_out_ref[place]).astype(bf16)
        held_rows[place * 2 + 1] = nt(pre, w_in_ref[place]).astype(bf16)
    x = place_ref[0] % 4
    for turn, out in enumerate((out0, out1, out2, out3)):
        out[...] = held_rows[(x + turn) % 4]
    own_slot_ref[...] = held_slots[x // 2]
    own_lse_ref[...] = held_lse[x // 2]


def second_sum_kernel(in0, in1, in2, in3, slot_ref, lse_ref, out_ref):
    row = in0[...].astype(f32) + in1[...].astype(f32) + in2[...].astype(f32) + in3[...].astype(f32)
    row = row.astype(bf16).astype(f32)
    shift = jnp.sum(slot_ref[...].astype(f32) * row, axis=1, keepdims=True)
    columns = in_lanes((shift * 0.0,) * 3 + pieces(shift))
    write_rows(out_ref, row, lse_ref[...] + columns)


def token_kernel(
    place_ref, got_ref, logits_ref, tok_ref, grad_ref,
    mix, rows, keep_ref, give_ref, halves, sums,
):
    slots, length = logits_ref.shape
    owners = 16
    held = slots // owners
    lses, shifts = [], []
    for place in range(held):
        first, extra = read_rows(got_ref, place * 2, owners)
        second, _ = read_rows(got_ref, 4 + place * 2, owners)
        rows[0, place * owners : (place + 1) * owners] = (first + second).astype(bf16)
        lses.append(from_lanes(extra, 0))
        first, extra_a = read_rows(got_ref, place * 2 + 1, owners)
        second, extra_b = read_rows(got_ref, 4 + place * 2 + 1, owners)
        rows[1, place * owners : (place + 1) * owners] = (first + second).astype(bf16)
        halves[place * owners : (place + 1) * owners] = first.astype(bf16)
        halves[slots + place * owners : slots + (place + 1) * owners] = second.astype(bf16)
        shifts.append(from_lanes(extra_a, 3) + from_lanes(extra_b, 3))
    lse = jnp.concatenate(lses, axis=0)
    shift = jnp.concatenate(shifts, axis=0)
    logits = logits_ref[...]
    probs = slot_softmax(logits)
    share = jnp.exp(logits - lse)
    mix[0] = probs.astype(bf16)
    mix[2] = share.astype(bf16)
    grad_probs = nt(rows[0], grad_ref[...])
    comb = probs * (grad_probs - jnp.sum(probs * grad_probs, axis=0, keepdims=True))
    inner = nt(halves[...], tok_ref[...])
    inner = inner[:slots] + inner[slots:]
    logit_grad = (comb + share * (inner - shift)).astype(bf16)
    mix[1] = logit_grad
    natural = tn(slot_order(owners, held), logit_grad).astype(bf16)
    total = nn(natural, tok_ref[...])
    half = slots // 2
    sums[0] = total[:half]
    sums[1] = total[half:]
    core = place_ref[0] // 4
    keep_ref[...] = sums[core]
    give_ref[...] = sums[1 - core]


def router_split_kernel(keep_ref, got_ref, out_ref):
    share = keep_ref.shape[1] // 8
    rows = out_ref.shape[1]
    total = keep_ref[...] + got_ref[...]
    for member in range(8):
        part = total[:, member * share : (member + 1) * share]
        packed = jnp.concatenate(
            [part[group * rows : (group + 1) * rows] for group in range(part.shape[0] // rows)],
            axis=1,
        ).astype(bf16)
        for copy in range(8):
            out_ref[member * 8 + copy] = packed


def router_sum_kernel(got_ref, out_ref):
    share = out_ref.shape[1]
    rows = got_ref.shape[1]
    total = got_ref[0].astype(f32)
    for member in range(1, got_ref.shape[0]):
        total = total + got_ref[member].astype(f32)
    for group in range(out_ref.shape[0] // rows):
        out_ref[group * rows : (group + 1) * rows] = total[:, group * share : (group + 1) * share]


def router_join_kernel(place_ref, half_ref, other_ref, out_ref):
    half = half_ref.shape[0]
    first = place_ref[0] // 4 == 0
    own, other = half_ref[...], other_ref[...]
    out_ref[:half] = jnp.where(first, own, other)
    out_ref[half:] = jnp.where(first, other, own)


def late_kernel(
    rows_ref, units_ref, mix_ref, back_ref, router_ref, w_in_ref, w_out_ref, mixed_ref, grad_ref,
    w_in, w_out, mixed, grad, sems, mix_sems,
):
    held, width, units = w_in.shape
    chunk = mixed.shape[0] // MIX_CHUNKS
    slots = back_ref.shape[1]

    def weight_copies(place):
        return [
            pltpu.make_async_copy(kept.at[place], ref.at[place], sems.at[2 * place + number])
            for number, (kept, ref) in enumerate(((w_out, w_out_ref), (w_in, w_in_ref)))
        ]

    def weight_step(place, carry):
        first, second = weight_copies(place)
        w_out[place] = tn(units_ref[place * 2], rows_ref[place * 2 + 1]).astype(bf16)
        first.start()
        w_in[place] = tn(rows_ref[place * 2], units_ref[place * 2 + 1]).astype(bf16)
        second.start()
        return carry

    def mix_copies(part):
        span = pl.ds(pl.multiple_of(part * chunk, chunk), chunk)
        return [
            pltpu.make_async_copy(kept.at[span, :], ref.at[span, :], mix_sems.at[2 * part + number])
            for number, (kept, ref) in enumerate(((mixed, mixed_ref), (grad, grad_ref)))
        ]

    def mix_step(part, carry):
        first, second = mix_copies(part)
        span = pl.ds(pl.multiple_of(part * chunk, chunk), chunk)
        mixed[span, :] = tn(mix_ref[0, :, span], back_ref[0]).astype(bf16)
        first.start()
        both = jnp.concatenate([mix_ref[1, :, span], mix_ref[2, :, span]], axis=0)
        grad[span, :] = tn(both, table).astype(bf16)
        second.start()
        return carry

    def wait(copies):
        def step(part, carry):
            for copy in copies(part):
                copy.wait()
            return carry

        return step

    table = jnp.concatenate([router_rows(router_ref, slots // held, held), back_ref[1]], axis=0)
    lax.fori_loop(0, held, weight_step, 0)
    lax.fori_loop(0, MIX_CHUNKS, mix_step, 0)
    lax.fori_loop(0, held, wait(weight_copies), 0)
    lax.fori_loop(0, MIX_CHUNKS, wait(mix_copies), 0)


def around_x(arrays):
    got = [arrays[0]]
    for turn in range(1, 4):
        pairs = [(place, (place + turn) % 4) for place in range(4)]
        got.append(lax.ppermute(arrays[turn], "x", pairs))
    return got


def params(mib):
    return pltpu.CompilerParams(vmem_limit_bytes=mib * MIB)


def per_device(tokens, router, w_in, w_out, grad_out):
    place = (lax.axis_index("x") + 4 * lax.axis_index("core")).astype(jnp.int32).reshape(1)
    tok = tokens[0]
    grad = grad_out[0]
    length, width = tok.shape
    router_t = router.T
    slots = router.shape[1]
    held, _, units = w_in.shape
    owners = slots // held
    wide = width + LANES
    sent = (8 * owners, 2, width // 2 + LANES)
    token_flops = 2 * length * width * slots
    expert_flops = 2 * held * owners * width * units

    *send, logits, tok_held, grad_held = pl.pallas_call(
        first_kernel,
        out_shape=[shape((owners, wide), f32)] * 4
        + [shape((slots, length), f32)]
        + [shape((length, width), bf16)] * 2,
        in_specs=[SMEM, HBM, VMEM, HBM],
        out_specs=[VMEM] * 7,
        scratch_shapes=[
            pltpu.VMEM((4, owners, wide), f32),
            pltpu.SemaphoreType.DMA((2 * CHUNKS,)),
        ],
        compiler_params=params(48),
        cost_estimate=cost(3 * token_flops, 4 * length * width),
        name="first",
    )(place, tok, router_t, grad)
    got = around_x(send)
    send = pl.pallas_call(
        first_sum_kernel,
        out_shape=shape(sent, f32),
        in_specs=[SMEM] + [VMEM] * 4,
        out_specs=VMEM,
        compiler_params=params(8),
        name="first_sum",
    )(place, *got)
    got = lax.all_to_all(send, ALL, 0, 0, tiled=True)
    *send, own_slot, own_lse, rows, units_held = pl.pallas_call(
        expert_kernel,
        out_shape=[shape((owners, width), bf16)] * 4
        + [shape((owners, width), f32), shape((owners, LANES), f32)]
        + [shape((2 * held, owners, width), bf16), shape((2 * held, owners, units), bf16)],
        in_specs=[SMEM] + [VMEM] * 3,
        out_specs=[VMEM] * 8,
        scratch_shapes=[
            pltpu.VMEM((4, owners, width), bf16),
            pltpu.VMEM((held, owners, LANES), f32),
            pltpu.VMEM((held, owners, width), f32),
        ],
        compiler_params=params(8),
        cost_estimate=cost(4 * expert_flops, 4 * held * width * units),
        name="experts",
    )(place, got, w_in, w_out)
    got = around_x(send)
    send = pl.pallas_call(
        second_sum_kernel,
        out_shape=shape(sent, bf16),
        in_specs=[VMEM] * 6,
        out_specs=VMEM,
        compiler_params=params(8),
        name="second_sum",
    )(*got, own_slot, own_lse)
    got = lax.all_to_all(send, ALL, 0, 0, tiled=True)
    mix, backs, keep, give = pl.pallas_call(
        token_kernel,
        out_shape=[shape((3, slots, length), bf16), shape((2, slots, width), bf16)]
        + [shape((slots // 2, width), f32)] * 2,
        in_specs=[SMEM] + [VMEM] * 4,
        out_specs=[VMEM] * 4,
        scratch_shapes=[
            pltpu.VMEM((2 * slots, width), bf16),
            pltpu.VMEM((2, slots // 2, width), f32),
        ],
        compiler_params=params(8),
        cost_estimate=cost(3 * token_flops, 4 * length * width),
        name="tokens",
    )(place, got, logits, tok_held, grad_held)
    swap = [(0, 1), (1, 0)]
    got = lax.ppermute(give, "core", swap)
    share = width // 8
    send = pl.pallas_call(
        router_split_kernel,
        out_shape=shape((64, 4, 4 * share), bf16),
        in_specs=[VMEM] * 2,
        out_specs=VMEM,
        compiler_params=params(8),
        name="router_split",
    )(keep, got)
    send, rows, units_held, mix, backs = lax.optimization_barrier(
        (send, rows, units_held, mix, backs)
    )
    got = lax.all_to_all(send, CHIPS, 0, 0, tiled=True)
    late_shapes = [(held, width, units), (held, units, width), (length, width), (length, width)]
    grad_w_in, grad_w_out, mixed, grad_tokens = pl.pallas_call(
        late_kernel,
        out_shape=[shape(dims, bf16) for dims in late_shapes],
        in_specs=[VMEM] * 5,
        out_specs=[HBM] * 4,
        scratch_shapes=[pltpu.VMEM(dims, bf16) for dims in late_shapes]
        + [
            pltpu.SemaphoreType.DMA((2 * held,)),
            pltpu.SemaphoreType.DMA((2 * MIX_CHUNKS,)),
        ],
        compiler_params=params(20),
        cost_estimate=cost(200 * expert_flops, 4 * length * width),
        name="late",
    )(rows, units_held, mix, backs, router_t)
    got, mixed, grad_tokens, grad_w_in, grad_w_out = lax.optimization_barrier(
        (got, mixed, grad_tokens, grad_w_in, grad_w_out)
    )
    half = pl.pallas_call(
        router_sum_kernel,
        out_shape=shape((slots // 2, share), f32),
        in_specs=[VMEM],
        out_specs=VMEM,
        compiler_params=params(8),
        name="router_sum",
    )(got)
    other = lax.ppermute(half, "core", swap)
    grad_router = pl.pallas_call(
        router_join_kernel,
        out_shape=shape((slots, share), f32),
        in_specs=[SMEM] + [VMEM] * 2,
        out_specs=VMEM,
        compiler_params=params(8),
        name="router_join",
    )(place, half, other)
    return (mixed[None], grad_tokens[None], grad_router.T, grad_w_in, grad_w_out)


def solution(mesh):
    fine = Mesh(mesh.devices.reshape(2, 4, 4, 2, 2), ALL)
    in_specs = (
        P(EXP, SEQ, None),
        P(),
        P(EXP, None, SEQ),
        P(EXP, SEQ, None),
        P(EXP, SEQ, None),
    )
    out_specs = (
        P(EXP, SEQ, None),
        P(EXP, SEQ, None),
        P(SEQ, None),
        P(EXP, None, SEQ),
        P(EXP, SEQ, None),
    )
    return jax.shard_map(
        per_device, mesh=fine, in_specs=in_specs, out_specs=out_specs, check_vma=False
    )
```

```python
import math

import jax
import jax.numpy as jnp
from jax import lax
from jax.experimental import pallas as pl
from jax.experimental.pallas import tpu as pltpu
from jax.sharding import Mesh, PartitionSpec as P

bf16 = jnp.bfloat16
f32 = jnp.float32
ALL = ("yh", "x", "z", "yl", "core")
SEQ = ("yh", "x")
EXP = ("z", "yl", "core")
CHIPS = ("yh", "x", "z", "yl")
LANES = 128
CHUNKS = 2
MIX_CHUNKS = 2
MIB = 1024 * 1024

VMEM = pl.BlockSpec(memory_space=pltpu.VMEM)
SMEM = pl.BlockSpec(memory_space=pltpu.SMEM)
HBM = pl.BlockSpec(memory_space=pltpu.HBM)


def nn(a, b):
    return jnp.dot(a, b, preferred_element_type=f32)


def nt(a, b):
    return lax.dot_general(a, b, (((1,), (1,)), ((), ())), preferred_element_type=f32)


def tn(a, b):
    return lax.dot_general(a, b, (((0,), (0,)), ((), ())), preferred_element_type=f32)


def shape(dims, dtype):
    return jax.ShapeDtypeStruct(dims, dtype)


def cost(flops, moved):
    return pl.CostEstimate(flops=flops, bytes_accessed=moved, transcendentals=0)


def pieces(value):
    high = value.astype(bf16).astype(f32)
    rest = value - high
    middle = rest.astype(bf16).astype(f32)
    return high, middle, rest - middle


def in_lanes(columns):
    rows = columns[0].shape[0]
    lane = lax.broadcasted_iota(jnp.int32, (rows, LANES), 1)
    result = jnp.zeros((rows, LANES), f32)
    for place, column in enumerate(columns):
        result = jnp.where(lane == place, column, result)
    return result


def from_lanes(block, first):
    lane = lax.broadcasted_iota(jnp.int32, block.shape, 1)
    kept = jnp.where((lane >= first) & (lane < first + 3), block, 0.0)
    return jnp.sum(kept, axis=1, keepdims=True)


def log_sum_exp(values):
    top = values[0]
    for value in values[1:]:
        top = jnp.maximum(top, value)
    total = jnp.exp(values[0] - top)
    for value in values[1:]:
        total = total + jnp.exp(value - top)
    return top + jnp.log(total)


def normal(value):
    return 0.5 * (1.0 + lax.erf(value * (1.0 / math.sqrt(2.0))))


def slot_order(owners, held):
    slots = owners * held
    row = lax.broadcasted_iota(jnp.int32, (slots, slots), 0)
    column = lax.broadcasted_iota(jnp.int32, (slots, slots), 1)
    return (column == (row % owners) * held + row // owners).astype(bf16)


def router_rows(router_ref, owners, held):
    return nn(slot_order(owners, held), router_ref[...]).astype(bf16)


def fetches(sources, targets, sems):
    copies = []
    for source, target in zip(sources, targets):
        chunk = source.shape[0] // CHUNKS
        for part in range(CHUNKS):
            rows = pl.ds(part * chunk, chunk)
            copies.append(
                pltpu.make_async_copy(
                    source.at[rows, :], target.at[rows, :], sems.at[len(copies)]
                )
            )
    for copy in copies:
        copy.start()
    return copies


def slot_softmax(logits):
    top = jnp.max(logits, axis=0, keepdims=True)
    raw = jnp.exp(logits - top)
    return raw / jnp.sum(raw, axis=0, keepdims=True)


def first_kernel(
    place_ref, tok_ref, router_ref, grad_ref, out0, out1, out2, out3, logits_ref, tok, grad,
    held_rows, sems,
):
    length, width = tok_ref.shape
    slots = router_ref.shape[0]
    owners = out0.shape[0]
    held = slots // owners
    chunk = length // CHUNKS
    copies = fetches((tok_ref, grad_ref), (tok, grad), sems)
    table = router_rows(router_ref, owners, held)
    for part in range(CHUNKS):
        copies[part].wait()
        rows = pl.ds(part * chunk, chunk)
        logits_ref[:, rows] = nt(table, tok[rows, :])
    logits = logits_ref[...]
    top = jnp.max(logits, axis=1, keepdims=True)
    raw = jnp.exp(logits - top)
    total = jnp.sum(raw, axis=1, keepdims=True)
    local_slot = nn(raw.astype(bf16), tok[...]) / total
    lse = top + jnp.log(total)
    probs = slot_softmax(logits).astype(bf16)
    for copy in copies[CHUNKS:]:
        copy.wait()
    local_grad = nn(probs, grad[...])
    columns = []
    for place in range(held):
        columns += pieces(lse[place * owners : (place + 1) * owners])
    extra = in_lanes(columns)
    for place in range(held):
        span = slice(place * owners, (place + 1) * owners)
        half = width // 2
        for side in range(2):
            quarter = place * 2 + side
            columns = slice(side * half, (side + 1) * half)
            held_rows[quarter, :, :half] = local_slot[span, columns]
            held_rows[quarter, :, half:width] = local_grad[span, columns]
            held_rows[quarter, :, width:] = extra
    x = place_ref[0] % 4
    for turn, out in enumerate((out0, out1, out2, out3)):
        out[...] = held_rows[(x + turn) % 4]


def write_rows(out_ref, row, extra):
    owners, width = row.shape
    half = width // 2
    halves = [
        jnp.concatenate([row[:, :half], extra], axis=1),
        jnp.concatenate([row[:, half:], extra], axis=1),
    ]
    both = jnp.stack(halves, axis=1).astype(out_ref.dtype)
    for member in range(out_ref.shape[0] // owners):
        out_ref[member * owners : (member + 1) * owners] = both


def read_rows(got_ref, member, owners):
    first = member * owners
    half = got_ref.shape[2] - LANES
    left = got_ref[first : first + owners, 0, :].astype(f32)
    right = got_ref[first : first + owners, 1, :].astype(f32)
    return jnp.concatenate([left[:, :half], right[:, :half]], axis=1), left[:, half:]


def first_sum_kernel(place_ref, in0, in1, in2, in3, out_ref):
    width = in0.shape[1] - LANES
    x = place_ref[0] % 4
    blocks = [ref[...].astype(f32) for ref in (in0, in1, in2, in3)]
    lses = []
    for block in blocks:
        extra = block[:, width:]
        lses.append(jnp.where(x // 2 == 0, from_lanes(extra, 0), from_lanes(extra, 3)))
    lse = log_sum_exp(lses)
    half = width // 2
    slot, grad = 0.0, 0.0
    for block, part in zip(blocks, lses):
        slot = slot + block[:, :half] * jnp.exp(part - lse)
        grad = grad + block[:, half:width]
    high = slot.astype(bf16).astype(f32)
    cut = out_ref.shape[2] - half
    both = jnp.stack(
        [
            jnp.concatenate([high, grad[:, :cut]], axis=1),
            jnp.concatenate([slot - high, grad[:, cut:], in_lanes(pieces(lse))], axis=1),
        ],
        axis=1,
    ).astype(bf16)
    owners = high.shape[0]
    for member in range(out_ref.shape[0] // owners):
        out_ref[member * owners : (member + 1) * owners] = both


def expert_kernel(
    place_ref, got_ref, w_in_ref, w_out_ref,
    out0, out1, out2, out3, own_slot_ref, own_lse_ref, rows_kept, units_kept,
    held_rows, held_lse, held_slots,
):
    held = w_in_ref.shape[0]
    owners = out0.shape[0]
    for place in range(held):
        rows, grads, lses = [], [], []
        half = w_in_ref.shape[1] // 2
        for y in range(2):
            slots, slot_grads = [], []
            for side in range(2):
                first = (y * 4 + place * 2 + side) * owners
                upper = got_ref[first : first + owners, 0, :].astype(f32)
                lower = got_ref[first : first + owners, 1, :].astype(f32)
                slots.append(upper[:, :half] + lower[:, :half])
                slot_grads += [upper[:, half:], lower[:, half:-LANES]]
            rows.append(jnp.concatenate(slots, axis=1))
            grads.append(jnp.concatenate(slot_grads, axis=1))
            lses.append(from_lanes(lower[:, -LANES:], 0))
        lse = log_sum_exp(lses)
        slot_full = rows[0] * jnp.exp(lses[0] - lse) + rows[1] * jnp.exp(lses[1] - lse)
        held_slots[place] = slot_full
        slot = slot_full.astype(bf16)
        slot_grad = (grads[0] + grads[1]).astype(bf16)
        rows_kept[place * 2] = slot
        rows_kept[place * 2 + 1] = slot_grad
        held_lse[place] = in_lanes(pieces(lse))
        activation = nn(slot, w_in_ref[place])
        hidden_grad = nt(slot_grad, w_out_ref[place])
        cumulative = normal(activation)
        density = jnp.exp(-0.5 * activation * activation) * (1.0 / math.sqrt(2.0 * math.pi))
        hidden = (activation * cumulative).astype(bf16)
        pre = (hidden_grad * (cumulative + activation * density)).astype(bf16)
        units_kept[place * 2] = hidden
        units_kept[place * 2 + 1] = pre
        held_rows[place * 2] = nn(hidden, w_out_ref[place]).astype(bf16)
        held_rows[place * 2 + 1] = nt(pre, w_in_ref[place]).astype(bf16)
    x = place_ref[0] % 4
    for turn, out in enumerate((out0, out1, out2, out3)):
        out[...] = held_rows[(x + turn) % 4]
    own_slot_ref[...] = held_slots[x // 2]
    own_lse_ref[...] = held_lse[x // 2]


def second_sum_kernel(in0, in1, in2, in3, slot_ref, lse_ref, out_ref):
    row = in0[...].astype(f32) + in1[...].astype(f32) + in2[...].astype(f32) + in3[...].astype(f32)
    row = row.astype(bf16).astype(f32)
    shift = jnp.sum(slot_ref[...].astype(f32) * row, axis=1, keepdims=True)
    columns = in_lanes((shift * 0.0,) * 3 + pieces(shift))
    write_rows(out_ref, row, lse_ref[...] + columns)


def token_kernel(
    place_ref, got_ref, logits_ref, tok_ref, grad_ref,
    mix, rows, keep_ref, give_ref, halves, sums,
):
    slots, length = logits_ref.shape
    owners = 16
    held = slots // owners
    lses, shifts = [], []
    for place in range(held):
        first, extra = read_rows(got_ref, place * 2, owners)
        second, _ = read_rows(got_ref, 4 + place * 2, owners)
        rows[0, place * owners : (place + 1) * owners] = (first + second).astype(bf16)
        lses.append(from_lanes(extra, 0))
        first, extra_a = read_rows(got_ref, place * 2 + 1, owners)
        second, extra_b = read_rows(got_ref, 4 + place * 2 + 1, owners)
        rows[1, place * owners : (place + 1) * owners] = (first + second).astype(bf16)
        halves[place * owners : (place + 1) * owners] = first.astype(bf16)
        halves[slots + place * owners : slots + (place + 1) * owners] = second.astype(bf16)
        shifts.append(from_lanes(extra_a, 3) + from_lanes(extra_b, 3))
    lse = jnp.concatenate(lses, axis=0)
    shift = jnp.concatenate(shifts, axis=0)
    logits = logits_ref[...]
    probs = slot_softmax(logits)
    share = jnp.exp(logits - lse)
    mix[0] = probs.astype(bf16)
    mix[2] = share.astype(bf16)
    grad_probs = nt(rows[0], grad_ref[...])
    comb = probs * (grad_probs - jnp.sum(probs * grad_probs, axis=0, keepdims=True))
    inner = nt(halves[...], tok_ref[...])
    inner = inner[:slots] + inner[slots:]
    logit_grad = (comb + share * (inner - shift)).astype(bf16)
    mix[1] = logit_grad
    natural = tn(slot_order(owners, held), logit_grad).astype(bf16)
    total = nn(natural, tok_ref[...])
    half = slots // 2
    sums[0] = total[:half]
    sums[1] = total[half:]
    core = place_ref[0] // 4
    keep_ref[...] = sums[core]
    give_ref[...] = sums[1 - core]


def router_split_kernel(keep_ref, got_ref, out_ref):
    share = keep_ref.shape[1] // 8
    rows = out_ref.shape[1]
    total = keep_ref[...] + got_ref[...]
    for member in range(8):
        part = total[:, member * share : (member + 1) * share]
        packed = jnp.concatenate(
            [part[group * rows : (group + 1) * rows] for group in range(part.shape[0] // rows)],
            axis=1,
        ).astype(bf16)
        for copy in range(8):
            out_ref[member * 8 + copy] = packed


def router_sum_kernel(got_ref, out_ref):
    share = out_ref.shape[1]
    rows = got_ref.shape[1]
    total = got_ref[0].astype(f32)
    for member in range(1, got_ref.shape[0]):
        total = total + got_ref[member].astype(f32)
    for group in range(out_ref.shape[0] // rows):
        out_ref[group * rows : (group + 1) * rows] = total[:, group * share : (group + 1) * share]


def router_join_kernel(place_ref, half_ref, other_ref, out_ref):
    half = half_ref.shape[0]
    first = place_ref[0] // 4 == 0
    own, other = half_ref[...], other_ref[...]
    out_ref[:half] = jnp.where(first, own, other)
    out_ref[half:] = jnp.where(first, other, own)


def late_kernel(
    rows_ref, units_ref, mix_ref, back_ref, router_ref, w_in_ref, w_out_ref, mixed_ref, grad_ref,
    w_in, w_out, mixed, grad, sems, mix_sems,
):
    held, width, units = w_in.shape
    chunk = mixed.shape[0] // MIX_CHUNKS
    slots = back_ref.shape[1]

    def weight_copies(place):
        return [
            pltpu.make_async_copy(kept.at[place], ref.at[place], sems.at[2 * place + number])
            for number, (kept, ref) in enumerate(((w_out, w_out_ref), (w_in, w_in_ref)))
        ]

    def weight_step(place, carry):
        first, second = weight_copies(place)
        w_out[place] = tn(units_ref[place * 2], rows_ref[place * 2 + 1]).astype(bf16)
        first.start()
        w_in[place] = tn(rows_ref[place * 2], units_ref[place * 2 + 1]).astype(bf16)
        second.start()
        return carry

    def mix_copies(part):
        span = pl.ds(pl.multiple_of(part * chunk, chunk), chunk)
        return [
            pltpu.make_async_copy(kept.at[span, :], ref.at[span, :], mix_sems.at[2 * part + number])
            for number, (kept, ref) in enumerate(((mixed, mixed_ref), (grad, grad_ref)))
        ]

    def mix_step(part, carry):
        first, second = mix_copies(part)
        span = pl.ds(pl.multiple_of(part * chunk, chunk), chunk)
        mixed[span, :] = tn(mix_ref[0, :, span], back_ref[0]).astype(bf16)
        first.start()
        both = jnp.concatenate([mix_ref[1, :, span], mix_ref[2, :, span]], axis=0)
        grad[span, :] = tn(both, table).astype(bf16)
        second.start()
        return carry

    def wait(copies):
        def step(part, carry):
            for copy in copies(part):
                copy.wait()
            return carry

        return step

    table = jnp.concatenate([router_rows(router_ref, slots // held, held), back_ref[1]], axis=0)
    lax.fori_loop(0, held, weight_step, 0)
    lax.fori_loop(0, MIX_CHUNKS, mix_step, 0)
    lax.fori_loop(0, held, wait(weight_copies), 0)
    lax.fori_loop(0, MIX_CHUNKS, wait(mix_copies), 0)


def around_x(arrays):
    got = [arrays[0]]
    for turn in range(1, 4):
        pairs = [(place, (place + turn) % 4) for place in range(4)]
        got.append(lax.ppermute(arrays[turn], "x", pairs))
    return got


def params(mib):
    return pltpu.CompilerParams(vmem_limit_bytes=mib * MIB)


def per_device(tokens, router, w_in, w_out, grad_out):
    place = (lax.axis_index("x") + 4 * lax.axis_index("core")).astype(jnp.int32).reshape(1)
    tok = tokens[0]
    grad = grad_out[0]
    length, width = tok.shape
    router_t = router.T
    slots = router.shape[1]
    held, _, units = w_in.shape
    owners = slots // held
    wide = width + LANES
    sent = (8 * owners, 2, width // 2 + LANES)
    token_flops = 2 * length * width * slots
    expert_flops = 2 * held * owners * width * units

    *send, logits, tok_held, grad_held = pl.pallas_call(
        first_kernel,
        out_shape=[shape((owners, wide), f32)] * 4
        + [shape((slots, length), f32)]
        + [shape((length, width), bf16)] * 2,
        in_specs=[SMEM, HBM, VMEM, HBM],
        out_specs=[VMEM] * 7,
        scratch_shapes=[
            pltpu.VMEM((4, owners, wide), f32),
            pltpu.SemaphoreType.DMA((2 * CHUNKS,)),
        ],
        compiler_params=params(48),
        cost_estimate=cost(3 * token_flops, 4 * length * width),
        name="first",
    )(place, tok, router_t, grad)
    got = around_x(send)
    send = pl.pallas_call(
        first_sum_kernel,
        out_shape=shape((8 * owners, 2, 8 * LANES), bf16),
        in_specs=[SMEM] + [VMEM] * 4,
        out_specs=VMEM,
        compiler_params=params(8),
        name="first_sum",
    )(place, *got)
    got = lax.all_to_all(send, ALL, 0, 0, tiled=True)
    *send, own_slot, own_lse, rows, units_held = pl.pallas_call(
        expert_kernel,
        out_shape=[shape((owners, width), bf16)] * 4
        + [shape((owners, width), f32), shape((owners, LANES), f32)]
        + [shape((2 * held, owners, width), bf16), shape((2 * held, owners, units), bf16)],
        in_specs=[SMEM] + [VMEM] * 3,
        out_specs=[VMEM] * 8,
        scratch_shapes=[
            pltpu.VMEM((4, owners, width), bf16),
            pltpu.VMEM((held, owners, LANES), f32),
            pltpu.VMEM((held, owners, width), f32),
        ],
        compiler_params=params(8),
        cost_estimate=cost(4 * expert_flops, 4 * held * width * units),
        name="experts",
    )(place, got, w_in, w_out)
    got = around_x(send)
    send = pl.pallas_call(
        second_sum_kernel,
        out_shape=shape(sent, bf16),
        in_specs=[VMEM] * 6,
        out_specs=VMEM,
        compiler_params=params(8),
        name="second_sum",
    )(*got, own_slot, own_lse)
    got = lax.all_to_all(send, ALL, 0, 0, tiled=True)
    mix, backs, keep, give = pl.pallas_call(
        token_kernel,
        out_shape=[shape((3, slots, length), bf16), shape((2, slots, width), bf16)]
        + [shape((slots // 2, width), f32)] * 2,
        in_specs=[SMEM] + [VMEM] * 4,
        out_specs=[VMEM] * 4,
        scratch_shapes=[
            pltpu.VMEM((2 * slots, width), bf16),
            pltpu.VMEM((2, slots // 2, width), f32),
        ],
        compiler_params=params(8),
        cost_estimate=cost(3 * token_flops, 4 * length * width),
        name="tokens",
    )(place, got, logits, tok_held, grad_held)
    swap = [(0, 1), (1, 0)]
    got = lax.ppermute(give, "core", swap)
    share = width // 8
    send = pl.pallas_call(
        router_split_kernel,
        out_shape=shape((64, 4, 4 * share), bf16),
        in_specs=[VMEM] * 2,
        out_specs=VMEM,
        compiler_params=params(8),
        name="router_split",
    )(keep, got)
    send, rows, units_held, mix, backs = lax.optimization_barrier(
        (send, rows, units_held, mix, backs)
    )
    got = lax.all_to_all(send, CHIPS, 0, 0, tiled=True)
    late_shapes = [(held, width, units), (held, units, width), (length, width), (length, width)]
    grad_w_in, grad_w_out, mixed, grad_tokens = pl.pallas_call(
        late_kernel,
        out_shape=[shape(dims, bf16) for dims in late_shapes],
        in_specs=[VMEM] * 5,
        out_specs=[HBM] * 4,
        scratch_shapes=[pltpu.VMEM(dims, bf16) for dims in late_shapes]
        + [
            pltpu.SemaphoreType.DMA((2 * held,)),
            pltpu.SemaphoreType.DMA((2 * MIX_CHUNKS,)),
        ],
        compiler_params=params(20),
        cost_estimate=cost(200 * expert_flops, 4 * length * width),
        name="late",
    )(rows, units_held, mix, backs, router_t)
    got, mixed, grad_tokens, grad_w_in, grad_w_out = lax.optimization_barrier(
        (got, mixed, grad_tokens, grad_w_in, grad_w_out)
    )
    half = pl.pallas_call(
        router_sum_kernel,
        out_shape=shape((slots // 2, share), f32),
        in_specs=[VMEM],
        out_specs=VMEM,
        compiler_params=params(8),
        name="router_sum",
    )(got)
    other = lax.ppermute(half, "core", swap)
    grad_router = pl.pallas_call(
        router_join_kernel,
        out_shape=shape((slots, share), f32),
        in_specs=[SMEM] + [VMEM] * 2,
        out_specs=VMEM,
        compiler_params=params(8),
        name="router_join",
    )(place, half, other)
    return (mixed[None], grad_tokens[None], grad_router.T, grad_w_in, grad_w_out)


def solution(mesh):
    fine = Mesh(mesh.devices.reshape(2, 4, 4, 2, 2), ALL)
    in_specs = (
        P(EXP, SEQ, None),
        P(),
        P(EXP, None, SEQ),
        P(EXP, SEQ, None),
        P(EXP, SEQ, None),
    )
    out_specs = (
        P(EXP, SEQ, None),
        P(EXP, SEQ, None),
        P(SEQ, None),
        P(EXP, None, SEQ),
        P(EXP, SEQ, None),
    )
    return jax.shard_map(
        per_device, mesh=fine, in_specs=in_specs, out_specs=out_specs, check_vma=False
    )
```
